128 devices in a mesh: sub: 16 (over z, x), blk: 8 (over y, core).
Axes of the slice: x: 4, y: 4, z: 4, core: 2. Of those that a mesh axis runs over, the one named last changes fastest.
Arguments:
- right_side: float32 [64, 2048, 512], P('sub', 'blk'), may hold values from -8 to 8
- trans_x: float32 [64, 2048, 512], P('sub', 'blk'), may hold values from 0.01 to 10
- trans_y: float32 [64, 2048, 512], P('sub', 'blk'), may hold values from 0.01 to 10
- trans_z: float32 [64, 2048, 512], P('sub', 'blk'), may hold values from 0.01 to 10
- storage: float32 [64, 2048, 512], P('sub', 'blk'), may hold values from 0.05 to 1
- pair_perm: int32 [16, 8, 1024], P('sub', 'blk'), may hold values from 0 to 1023, each once within a row
- pair_type: int32 [16, 8, 1024], P('sub', 'blk'), may hold values from 0 to 3
- pair_count: int32 [16, 8], P('sub', 'blk'), may hold values from 256 to 1024
- proj: float32 [4, 128, 128], replicated, may hold values from -1 to 2, as said below
Outputs:
- solution_field: float32 [64, 2048, 512], P('sub', 'blk')
- residual: float32 [64, 2048, 512], P('sub', 'blk')
The draws below stay inside these ranges and needn't reach their ends.
Inputs may be any that keep to these rules, and one draw needn't show every extreme that they name: `pair_perm`: each subdomain's list is a permutation of its face blocks. `proj`: projection matrices of order one.
All inputs are finite; a program needn't handle non-finite values.
Results may differ from the reference program's by a relative error of at most 0.00013.
Values sent between devices are 32-bit elements; how exact they have to be, the bound alone decides.
A program may use at most 128 MiB of HBM per device.

```python
import math
import jax
import jax.numpy as jnp
from jax import lax

CX = 4
CY = 256
CZ = 512
FB = 128
NPROJ = 4
ITERS = 2
NFB = 1024
NX = 64
NY = 2048
NZ = 512
N_SUB = 16
N_BLK = 8


def draw_proj(key, part):
    key = jax.random.fold_in(key, 7)
    noise = jax.random.normal(key, (NPROJ, FB, FB), jnp.float32)
    noise = jnp.clip(noise, -5.0, 5.0)
    return jnp.eye(FB, dtype=jnp.float32)[None] + 0.4 / FB ** 0.5 * noise


def plant(entries, own_key, low, top_value):
    longest = entries.shape.index(max(entries.shape))
    spots = []
    for shift in (0, 1):
        where = [jax.random.randint(jax.random.fold_in(own_key, axis), (), 0, length) for axis, length in enumerate(entries.shape)]
        where[longest] = (where[longest] + shift) % entries.shape[longest]
        spots.append(tuple(where))
    return entries.at[spots[0]].set(low).at[spots[1]].set(top_value)


def block_levels(rng, extent, pieces, smallest, top_value):
    def one(position, blocks):
        steps = jax.random.uniform(jax.random.fold_in(jax.random.fold_in(rng, 6), position), (blocks,), jnp.float32, smallest / len(pieces), top_value / len(pieces))
        return jnp.repeat(jnp.exp(steps), extent[position] // blocks).reshape((-1,) + (1,) * (len(extent) - position - 1))

    loudness = one(*pieces[0])
    for cut in pieces[1:]:
        loudness = loudness * one(*cut)
    return loudness


def bell_draw(key, dims, scale, most, shards=(), held_as=jnp.bfloat16):
    entries = jax.random.normal(key, dims, jnp.float32) * scale
    if len(shards) > 0:
        entries = block_levels(key, dims, shards, -0.22, 0.18) * entries
    return jnp.clip(entries, min=-most, max=most).astype(held_as)


def setup_inputs(seed: int = 0) -> dict:
    keys = jax.random.split(jax.random.key(seed), 10)
    return {
        "right_side": bell_draw(keys[0], (NX, NY, NZ), 1.0, 8.0, ((0, 16), (1, 8)), jnp.float32),
        "trans_x": jnp.clip(jnp.exp(math.log(10.0) - 6.9077553 * jax.random.uniform(keys[1], (NX, NY, NZ), jnp.float32) ** block_levels(keys[1], (NX, NY, NZ), ((0, 16), (1, 8)), -0.2, 0.2)), 0.01, 10.0),
        "trans_y": jnp.clip(jnp.exp(math.log(10.0) - 6.9077553 * jax.random.uniform(keys[2], (NX, NY, NZ), jnp.float32) ** block_levels(keys[2], (NX, NY, NZ), ((0, 16), (1, 8)), -0.2, 0.2)), 0.01, 10.0),
        "trans_z": jnp.clip(jnp.exp(math.log(10.0) - 6.9077553 * jax.random.uniform(keys[3], (NX, NY, NZ), jnp.float32) ** block_levels(keys[3], (NX, NY, NZ), ((0, 16), (1, 8)), -0.2, 0.2)), 0.01, 10.0),
        "storage": jnp.clip(jnp.exp(math.log(1.0) - 2.9957323 * jax.random.uniform(keys[4], (NX, NY, NZ), jnp.float32) ** block_levels(keys[4], (NX, NY, NZ), ((0, 16), (1, 8)), -0.2, 0.2)), 0.05, 1.0),
        "pair_perm": jax.vmap(lambda own: jax.random.permutation(own, NFB))(jax.random.split(keys[5], N_SUB * N_BLK)).reshape((N_SUB, N_BLK, NFB)).astype(jnp.int32),
        "pair_type": plant(jax.random.randint(keys[6], (N_SUB, N_BLK, NFB), 0, NPROJ), jax.random.fold_in(keys[6], 1), 0, NPROJ - 1).astype(jnp.int32),
        "pair_count": plant(jax.random.randint(keys[7], (N_SUB, N_BLK), NFB // 4, NFB + 1), jax.random.fold_in(keys[7], 1), NFB // 4, NFB).astype(jnp.int32),
        "proj": draw_proj(jax.random.fold_in(keys[9], 71), 0),
    }


penalty = 4.0


def shift_next(values, axis):
    count = values.shape[axis]
    rest = lax.slice_in_dim(values, 1, count, axis=axis)
    return jnp.concatenate([rest, jnp.zeros_like(lax.slice_in_dim(values, 0, 1, axis=axis))], axis)


def shift_prev(values, axis):
    count = values.shape[axis]
    rest = lax.slice_in_dim(values, 0, count - 1, axis=axis)
    return jnp.concatenate([jnp.zeros_like(lax.slice_in_dim(values, 0, 1, axis=axis)), rest], axis)


def operate(field, coeffs, storage, pair_perm, pair_type, live, proj):
    result = storage * field
    for axis in range(3):
        coeff = coeffs[axis]
        result = result + coeff * (field - shift_next(field, axis)) + shift_prev(coeff, axis) * (field - shift_prev(field, axis))
    view = field.reshape(N_SUB, CX, N_BLK, CY, CZ)
    last = view[:, CX - 1].reshape(N_SUB, N_BLK, NFB, FB)
    first = view[:, 0].reshape(N_SUB, N_BLK, NFB, FB)
    right = jnp.concatenate([first[1:], jnp.zeros_like(first[:1])], 0)
    gathered = jnp.take_along_axis(right, pair_perm[..., None], axis=2)
    projected = jnp.zeros_like(last)
    for kind in range(NPROJ):
        select = (pair_type == kind).astype(jnp.float32)[..., None]
        projected = projected + select * jnp.einsum("sbkc,ac->sbka", gathered, proj[kind], precision=lax.Precision.HIGHEST)
    jump = live[..., None] * (last - projected)
    back = jnp.zeros_like(last)
    for kind in range(NPROJ):
        select = (pair_type == kind).astype(jnp.float32)[..., None]
        back = back + select * jnp.einsum("sbka,ac->sbkc", jump, proj[kind], precision=lax.Precision.HIGHEST)
    back = -penalty * back
    sub_index = jnp.arange(N_SUB, dtype=jnp.int32)[:, None, None]
    blk_index = jnp.arange(N_BLK, dtype=jnp.int32)[None, :, None]
    ordered = jnp.zeros_like(back).at[sub_index, blk_index, pair_perm].set(back)
    received = jnp.concatenate([jnp.zeros_like(ordered[:1]), ordered[:-1]], 0)
    extra = jnp.zeros((N_SUB, CX, N_BLK, CY, CZ), jnp.float32)
    extra = extra.at[:, CX - 1].add((penalty * jump).reshape(N_SUB, N_BLK, CY, CZ))
    extra = extra.at[:, 0].add(received.reshape(N_SUB, N_BLK, CY, CZ))
    return result + extra.reshape(NX, NY, NZ)


def reference(right_side, trans_x, trans_y, trans_z, storage, pair_perm, pair_type, pair_count, proj):
    x_index = jnp.arange(NX, dtype=jnp.int32)[:, None, None]
    y_index = jnp.arange(NY, dtype=jnp.int32)[None, :, None]
    z_index = jnp.arange(NZ, dtype=jnp.int32)[None, None, :]
    tx = trans_x * (x_index % CX != CX - 1).astype(jnp.float32)
    ty = trans_y * (y_index != NY - 1).astype(jnp.float32)
    tz = trans_z * (z_index != NZ - 1).astype(jnp.float32)
    coeffs = (tx, ty, tz)
    live = (jnp.arange(NFB, dtype=jnp.int32)[None, None, :] < pair_count[..., None]).astype(jnp.float32)
    solution_field = jnp.zeros_like(right_side)
    residual, direction = right_side, right_side
    norm_now = jnp.sum(residual * residual)
    for step in range(ITERS):
        image = operate(direction, coeffs, storage, pair_perm, pair_type, live, proj)
        alpha = norm_now / jnp.sum(direction * image)
        solution_field = solution_field + alpha * direction
        residual = residual - alpha * image
        norm_next = jnp.sum(residual * residual)
        direction = residual + (norm_next / norm_now) * direction
        norm_now = norm_next
    return solution_field, residual
```

```python
import functools

import jax
import jax.numpy as jnp
from jax import lax
from jax.experimental import pallas as pl
from jax.experimental.pallas import tpu as pltpu
from jax.sharding import PartitionSpec as P

MESH = pl.DeviceIdType.MESH
F32, BF16, I32 = jnp.float32, jnp.bfloat16, jnp.int32
CX, CY, CZ = 4, 256, 512
FB, KINDS = 128, 4
GROUPS = CZ // FB
NFB = CY * GROUPS
PAD = 8
ROWS = 32
PENALTY = 4.0


def split(x):
    high = x.astype(BF16)
    low = (x - high.astype(F32)).astype(BF16)
    return jnp.concatenate([high, low], axis=1)


def fold(x):
    total = None
    for r in range(0, x.shape[0], 8):
        for c in range(0, x.shape[1], 128):
            tile = x[r : r + 8, c : c + 128]
            total = tile if total is None else total + tile
    return total


def choose(y, kind):
    out = y[:, (KINDS - 1) * FB :]
    for t in range(KINDS - 2, -1, -1):
        out = jnp.where(kind == t, y[:, t * FB : (t + 1) * FB], out)
    return out


def project(pair, double, single, kind):
    y = jnp.dot(pair, double[...], preferred_element_type=F32)
    y = y + jnp.dot(pair[:, :FB], single[...], preferred_element_type=F32)
    return choose(y, kind)


def kernel(n_sub, n_blk, b_hbm, tx_hbm, ty_hbm, tz_hbm, st_hbm, perm_hbm, type_hbm, count_hbm, proj_hbm,
           x_ref, r_ref,
           B, TX, TY, TZ, ST, W, V,
           perm_v, type_v, count_s, meta, meta_in, PROJ,
           pt2, pt1, pp2, pp1, CB, NAT, GL, GR, GT,
           face_in, last_in, sl, sl_in, sf, psf, psf_in,
           HL, HL2, J1L, C2L, J1R, C2R, Q2,
           cur, slots,
           load_sem, small_sem, ss, rs, ar_ss, ar_rs):
    s, k = lax.axis_index("sub"), lax.axis_index("blk")
    right, left = (lax.rem(s + 1, n_sub), k), (lax.rem(s + n_sub - 1, n_sub), k)
    up, down = (s, lax.rem(k + 1, n_blk)), (s, lax.rem(k + n_blk - 1, n_blk))
    column = [(lax.rem(s + i, n_sub), k) for i in range(1, n_sub)]
    row = [(s, lax.rem(k + i, n_blk)) for i in range(1, n_blk)]

    barrier = pltpu.get_barrier_semaphore()
    for peer in [column[0], column[-1], row[0], row[-1]] + column[1:-1] + row[1:-1]:
        pl.semaphore_signal(barrier, inc=1, device_id=peer, device_id_type=MESH)

    small = [
        pltpu.make_async_copy(perm_hbm, perm_v, small_sem.at[0]),
        pltpu.make_async_copy(type_hbm, type_v, small_sem.at[1]),
        pltpu.make_async_copy(count_hbm, count_s, small_sem.at[2]),
        pltpu.make_async_copy(proj_hbm, PROJ, small_sem.at[3]),
    ]
    for c in small:
        c.start()

    def load(a, i):
        src, dst = ((b_hbm, B), (tx_hbm, TX), (ty_hbm, TY), (tz_hbm, TZ), (st_hbm, ST))[a]
        to = dst.at[i, pl.ds(PAD, CY), :] if a in (0, 2) else dst.at[i]
        return pltpu.make_async_copy(src.at[i], to, load_sem.at[a, i])

    order = [(0, 3), (0, 2), (2, 3), (3, 3), (4, 3), (1, 2), (0, 0), (0, 1), (2, 0), (3, 0), (4, 0), (1, 0),
             (2, 1), (3, 1), (4, 1), (1, 1), (2, 2), (3, 2), (4, 2)]
    for a, i in order:
        load(a, i).start()

    pl.semaphore_wait(barrier, n_sub + n_blk - 2)

    def send(src, dst, n, to):
        return pltpu.make_async_remote_copy(
            src_ref=src, dst_ref=dst, send_sem=ss.at[n], recv_sem=rs.at[n], device_id=to, device_id_type=MESH
        )

    b_up = send(b_hbm.at[:, CY - 1 : CY, :], B.at[:, PAD - 1 : PAD, :], 0, up)
    b_down = send(b_hbm.at[:, 0:1, :], B.at[:, PAD + CY : PAD + CY + 1, :], 1, down)
    ty_up = send(ty_hbm.at[:, CY - 1 : CY, :], TY.at[:, PAD - 1 : PAD, :], 2, up)
    meta_right = send(meta, meta_in, 3, right)
    first_left = send(b_hbm.at[0], face_in, 4, left)
    last_right = send(b_hbm.at[CX - 1], last_in, 5, right)
    w_up = send(W.at[:, PAD + CY - 1 : PAD + CY, :], W.at[:, PAD - 1 : PAD, :], 6, up)
    w_down = send(W.at[:, PAD : PAD + 1, :], W.at[:, PAD + CY : PAD + CY + 1, :], 7, down)
    sl_right = [send(sl.at[pl.ds(q * CY, CY)], sl_in.at[pl.ds(q * CY, CY)], 8 + q, right) for q in range(GROUPS)]
    psf_left = [send(psf.at[pl.ds(q * CY, CY)], psf_in.at[pl.ds(q * CY, CY)], 12 + q, left) for q in range(GROUPS)]

    b_up.start()
    b_down.start()
    ty_up.start()
    first_left.start()
    last_right.start()

    for c in small:
        c.wait()
    meta[0:1, :] = perm_v[0]
    meta[1:2, :] = type_v[0]
    meta[2:3, :] = jnp.full((1, NFB), count_s[0, 0], I32)
    meta[3:8, :] = jnp.zeros((5, NFB), I32)
    meta_right.start()

    for t in range(KINDS):
        for source, double, single in ((PROJ[t].T, pt2, pt1), (PROJ[t], pp2, pp1)):
            high = source.astype(BF16)
            low = (source - high.astype(F32)).astype(BF16)
            at = slice(t * FB, (t + 1) * FB)
            double[0:FB, at] = high
            double[FB : 2 * FB, at] = high
            single[:, at] = low

    lane = lax.broadcasted_iota(I32, (FB, FB), 1)
    sub_row = lax.broadcasted_iota(I32, (FB, FB), 0)

    def columns_of(m, side):
        perm = m[0:1, :]
        place = jnp.bitwise_and(perm, GROUPS - 1) * CY + lax.shift_right_logical(perm, 2)
        live = (lax.broadcasted_iota(I32, (1, NFB), 1) < m[2:3, :]).astype(I32)
        code = (place + m[1:2, :] * NFB + live * (NFB * KINDS)).astype(F32)
        for i in range(NFB // FB):
            part = jnp.broadcast_to(code[:, i * FB : (i + 1) * FB], (FB, FB))
            NAT[i * FB : (i + 1) * FB, :] = part.T
        for q in range(GROUPS):
            CB[side, q * CY : (q + 1) * CY, :] = NAT[pl.ds(q, CY, stride=GROUPS), :].astype(I32)

    def one_hot(side, G):
        def step(i, _):
            r = pl.multiple_of(i * FB, FB)
            place = jnp.bitwise_and(CB[side, pl.ds(r, FB), :], NFB - 1)
            for j in range(NFB // FB):
                G[pl.ds(r, FB), j * FB : (j + 1) * FB] = jnp.where(place == lane + j * FB, 1.0, 0.0).astype(BF16)
            return 0
        lax.fori_loop(0, NFB // FB, step, 0)

    def one_hot_back(side, G):
        for i in range(NFB // FB):
            place = jnp.bitwise_and(CB[side, i * FB : (i + 1) * FB, :], NFB - 1).astype(F32).T.astype(I32)
            def step(j, _):
                r = pl.multiple_of(j * FB, FB)
                G[pl.ds(r, FB), i * FB : (i + 1) * FB] = jnp.where(place == sub_row + r, 1.0, 0.0).astype(BF16)
                return 0
            lax.fori_loop(0, NFB // FB, step, 0)

    def kind_of(side, r):
        return jnp.bitwise_and(lax.shift_right_logical(CB[side, pl.ds(r, CY), :], 10), KINDS - 1)

    def live_of(side, r):
        return lax.shift_right_logical(CB[side, pl.ds(r, CY), :], 12).astype(F32)

    columns_of(meta, 0)
    one_hot(0, GL)

    def stencil(S, i, c):
        y = pl.multiple_of(c * ROWS, ROWS)
        here = pl.ds(y, ROWS)
        big = S[i, pl.ds(y, ROWS + 2 * PAD), :]
        mid = big[PAD : PAD + ROWS]
        after = pltpu.roll(big, ROWS + 2 * PAD - 1, 0)
        flux = TY[i, pl.ds(y, ROWS + PAD), :] * (big[: PAD + ROWS] - after[: PAD + ROWS])
        out = ST[i, here, :] * mid + (flux[PAD:] - pltpu.roll(flux, 1, 0)[PAD:])
        flux = TZ[i, here, :] * (mid - pltpu.roll(mid, CZ - 1, 1))
        out = out + (flux - pltpu.roll(flux, 1, 1))
        inner = pl.ds(pl.multiple_of(y + PAD, PAD), ROWS)
        if i < CX - 1:
            out = out + TX[i, here, :] * (mid - S[i + 1, inner, :])
        if i > 0:
            out = out - TX[i - 1, here, :] * (S[i - 1, inner, :] - mid)
        return mid, out, inner, here

    def prepare(i):
        edge = TZ[i, :, CZ - FB :]
        TZ[i, :, CZ - FB :] = jnp.where(lax.broadcasted_iota(I32, (CY, FB), 1) == FB - 1, 0.0, edge)
        TY[i, PAD + CY - 1 : PAD + CY, :] = jnp.where(k < n_blk - 1, TY[i, PAD + CY - 1 : PAD + CY, :], 0.0)
        TY[i, PAD - 1 : PAD, :] = jnp.where(k > 0, TY[i, PAD - 1 : PAD, :], 0.0)

    for a, i in order[:6]:
        load(a, i).wait()
    b_up.wait_recv()
    b_down.wait_recv()
    ty_up.wait_recv()
    prepare(3)

    def last_face(c, _):
        mid, out, inner, here = stencil(B, 3, c)
        W[3, inner, :] = out
        for q in range(GROUPS):
            sl[pl.ds(pl.multiple_of(q * CY + c * ROWS, ROWS), ROWS), :] = out[:, q * FB : (q + 1) * FB]
        return 0

    lax.fori_loop(0, CY // ROWS, last_face, 0)
    for q in (2, 3, 0, 1):
        sl_right[q].start()

    for a, i in order[6:12]:
        load(a, i).wait()
    prepare(0)

    def first_face(c, _):
        mid, out, inner, here = stencil(B, 0, c)
        W[0, inner, :] = out
        for q in range(GROUPS):
            at = pl.ds(pl.multiple_of(q * CY + c * ROWS, ROWS), ROWS)
            cols = slice(q * FB, (q + 1) * FB)
            HL[at, :] = split(mid[:, cols])
            HL2[at, :] = split(out[:, cols])
        return 0

    lax.fori_loop(0, CY // ROWS, first_face, 0)

    meta_right.wait_recv()
    columns_of(meta_in, 1)
    one_hot(1, GR)

    def gather_first(q, _):
        r = pl.multiple_of(q * CY, CY)
        at = pl.ds(r, CY)
        kind = kind_of(1, r)
        g = jnp.dot(GR[at, :], HL2[...], preferred_element_type=F32)
        psf[at, :] = project(g.astype(BF16), pt2, pt1, kind)
        g = jnp.dot(GR[at, :], HL[...], preferred_element_type=F32)
        J1R[at, :] = project(g.astype(BF16), pt2, pt1, kind)
        return 0

    lax.fori_loop(0, GROUPS, gather_first, 0)
    for q in (0, 1, 2, 3):
        psf_left[q].start()

    one_hot_back(1, GT)

    for a, i in order[12:]:
        load(a, i).wait()
    zero = jnp.zeros((8, 128), F32)
    sums = (zero, zero, zero)
    for i in (1, 2):
        prepare(i)

        def middle(c, acc, i=i):
            mid, out, inner, here = stencil(B, i, c)
            W[i, inner, :] = out
            return acc[0] + fold(mid * mid), acc[1] + fold(mid * out), acc[2] + fold(out * out)

        sums = lax.fori_loop(0, CY // ROWS, middle, sums)

    has_right = (s < n_sub - 1).astype(F32)
    has_left = (s > 0).astype(F32)
    first_left.wait_recv()
    for q in range(GROUPS):
        HL[q * CY : (q + 1) * CY, :] = split(face_in[:, q * FB : (q + 1) * FB] * has_right)

    def last_jump(q, acc):
        r = pl.multiple_of(q * CY, CY)
        at, cols = pl.ds(r, CY), pl.ds(pl.multiple_of(q * FB, FB), FB)
        kind, live = kind_of(0, r), live_of(0, r)
        g = jnp.dot(GL[at, :], HL[...], preferred_element_type=F32).astype(BF16)
        mid = B[3, pl.ds(PAD, CY), cols]
        jump = live * (mid - project(g, pt2, pt1, kind))
        w = W[3, pl.ds(PAD, CY), cols] + PENALTY * jump
        W[3, pl.ds(PAD, CY), cols] = w
        back = project(split(jump), pp2, pp1, kind)
        C2L[at, :] = w + (PENALTY * has_right) * project(split(back), pt2, pt1, kind)
        return acc[0] + fold(mid * mid), acc[1] + fold(mid * w), acc[2] + fold(w * w)

    sums = lax.fori_loop(0, GROUPS, last_jump, sums)

    last_right.wait_recv()

    def first_jump(q, _):
        r = pl.multiple_of(q * CY, CY)
        at, cols = pl.ds(r, CY), pl.ds(pl.multiple_of(q * FB, FB), FB)
        kind, live = kind_of(1, r), live_of(1, r)
        jump = has_left * live * (last_in[:, cols] - J1R[at, :])
        back = project(split(jump), pp2, pp1, kind)
        HL2[at, :] = split(back)
        C2R[at, :] = PENALTY * jump - psf[at, :] + PENALTY * project(split(back), pt2, pt1, kind)
        return 0

    lax.fori_loop(0, GROUPS, first_jump, 0)

    def first_back(q, acc):
        at, cols = pl.ds(pl.multiple_of(q * CY, CY), CY), pl.ds(pl.multiple_of(q * FB, FB), FB)
        g = jnp.dot(GT[at, :], HL2[...], preferred_element_type=F32)
        w = W[0, pl.ds(PAD, CY), cols] - PENALTY * (g[:, :FB] + g[:, FB:])
        W[0, pl.ds(PAD, CY), cols] = w
        mid = B[0, pl.ds(PAD, CY), cols]
        return acc[0] + fold(mid * mid), acc[1] + fold(mid * w), acc[2] + fold(w * w)

    sums = lax.fori_loop(0, GROUPS, first_back, sums)

    w_up.start()
    w_down.start()

    def second(c, acc):
        for i in range(CX):
            mid, out, inner, here = stencil(W, i, c)
            V[i, here, :] = out
            acc = acc + fold(mid * out)
        return acc

    wv = lax.fori_loop(1, CY // ROWS - 1, second, zero)
    w_up.wait_recv()
    w_down.wait_recv()
    wv = second(0, wv)
    wv = second(CY // ROWS - 1, wv)

    def left_second(q):
        at, cols = slice(q * CY, (q + 1) * CY), slice(q * FB, (q + 1) * FB)
        psf_left[q].wait_recv()
        jump = live_of(0, q * CY) * (C2L[at, :] - has_right * psf_in[at, :])
        V[3, :, cols] = V[3, :, cols] + PENALTY * jump
        return fold(jump * jump)

    def right_second(q):
        at = slice(q * CY, (q + 1) * CY)
        sl_right[q].wait_recv()
        jump = has_left * live_of(1, q * CY) * (sl_in[at, :] + C2R[at, :])
        Q2[...] = split(project(split(jump), pp2, pp1, kind_of(1, q * CY)))

        def back(p, _):
            rows, cols = pl.ds(pl.multiple_of(p * CY, CY), CY), pl.ds(pl.multiple_of(p * FB, FB), FB)
            g = jnp.dot(GT[rows, at], Q2[...], preferred_element_type=F32)
            V[0, :, cols] = V[0, :, cols] - PENALTY * (g[:, :FB] + g[:, FB:])
            return 0

        lax.fori_loop(0, GROUPS, back, 0)
        return fold(jump * jump)

    no_right = 1.0 - has_right
    mortar = zero
    for q in (2, 3):
        only = live_of(0, q * CY) * C2L[q * CY : (q + 1) * CY, :]
        mortar = mortar + no_right * fold(only * only)
    mortar = mortar + left_second(0) + right_second(2) + left_second(1) + right_second(3)
    wv = wv + PENALTY * mortar

    lane_row = lax.broadcasted_iota(I32, (1, 128), 1)
    packed = jnp.zeros((1, 128), F32)
    for n, part in enumerate((sums[0], sums[1], sums[2], wv)):
        packed = jnp.where(lane_row == n, jnp.sum(part), packed)
    cur[0, 0:1, :] = packed

    def spread(stage, peers):
        out = []
        for i, peer in enumerate(peers):
            c = pltpu.make_async_remote_copy(
                src_ref=cur.at[stage, 0:1], dst_ref=slots.at[stage, i : i + 1],
                send_sem=ar_ss.at[stage], recv_sem=ar_rs.at[stage], device_id=peer, device_id_type=MESH,
            )
            c.start()
        return len(peers)

    def collect(stage, count):
        arrived = slots.at[stage, 0:count]
        pltpu.make_async_copy(arrived, arrived, ar_rs.at[stage]).wait()
        return cur[stage, 0:1, :] + jnp.sum(slots[stage, 0:count, :], axis=0, keepdims=True)

    n0 = spread(0, column)
    left_second(2)
    right_second(0)
    cur[1, 0:1, :] = collect(0, n0)
    n1 = spread(1, row)
    left_second(3)
    right_second(1)
    total = collect(1, n1)

    bb, bw, ww, wv = (total[0:1, n : n + 1] for n in range(4))
    alpha = bb / bw
    rr = alpha * alpha * ww - bb
    beta = rr / bb
    curve = bw - 2.0 * alpha * ww + alpha * alpha * wv - beta * beta * bw
    alpha2 = rr / curve
    first = alpha + alpha2 * (1.0 + beta)
    cross = alpha * alpha2

    def finish(c, _):
        y = pl.multiple_of(c * ROWS, ROWS)
        here, inner = pl.ds(y, ROWS), pl.ds(pl.multiple_of(y + PAD, PAD), ROWS)
        for i in range(CX):
            b, w = B[i, inner, :], W[i, inner, :]
            x_ref[i, here, :] = first * b - cross * w
            r_ref[i, here, :] = b - first * w + cross * V[i, here, :]
        return 0

    lax.fori_loop(0, CY // ROWS, finish, 0)

    for c in [b_up, b_down, ty_up, meta_right, first_left, last_right, w_up, w_down] + sl_right + psf_left:
        c.wait_send()
    for stage, count in ((0, n0), (1, n1)):
        sent = slots.at[stage, 0:count]
        pltpu.make_async_copy(sent, sent, ar_ss.at[stage]).wait()


def body(mesh, b, tx, ty, tz, st, perm, kind, count, proj):
    n_sub, n_blk = mesh.shape["sub"], mesh.shape["blk"]
    vm = lambda *shape, dtype=F32: pltpu.VMEM(shape, dtype)
    face = (NFB, FB)
    scratch = [
        vm(CX, CY + 2 * PAD, CZ), vm(CX, CY, CZ), vm(CX, CY + PAD, CZ), vm(CX, CY, CZ), vm(CX, CY, CZ),
        vm(CX, CY + 2 * PAD, CZ), vm(CX, CY, CZ),
        vm(1, 1, NFB, dtype=I32), vm(1, 1, NFB, dtype=I32), pltpu.SMEM((1, 1), I32),
        vm(8, NFB, dtype=I32), vm(8, NFB, dtype=I32), vm(KINDS, FB, FB),
        vm(2 * FB, KINDS * FB, dtype=BF16), vm(FB, KINDS * FB, dtype=BF16),
        vm(2 * FB, KINDS * FB, dtype=BF16), vm(FB, KINDS * FB, dtype=BF16),
        vm(2, NFB, FB, dtype=I32), vm(NFB, FB),
        vm(NFB, NFB, dtype=BF16), vm(NFB, NFB, dtype=BF16), vm(NFB, NFB, dtype=BF16),
        vm(CY, CZ), vm(CY, CZ), vm(*face), vm(*face), vm(*face), vm(*face), vm(*face),
        vm(NFB, 2 * FB, dtype=BF16), vm(NFB, 2 * FB, dtype=BF16), vm(*face), vm(*face), vm(*face), vm(*face),
        vm(CY, 2 * FB, dtype=BF16),
        vm(2, 8, 128), vm(2, 16, 128),
        pltpu.SemaphoreType.DMA((5, CX)), pltpu.SemaphoreType.DMA((4,)),
        pltpu.SemaphoreType.DMA((16,)), pltpu.SemaphoreType.DMA((16,)),
        pltpu.SemaphoreType.DMA((2,)), pltpu.SemaphoreType.DMA((2,)),
    ]
    out = jax.ShapeDtypeStruct((CX, CY, CZ), F32)
    return tuple(pl.pallas_call(
        functools.partial(kernel, n_sub, n_blk),
        out_shape=(out, out),
        in_specs=[pl.BlockSpec(memory_space=pl.ANY)] * 9,
        out_specs=(pl.BlockSpec(memory_space=pltpu.VMEM),) * 2,
        scratch_shapes=scratch,
        compiler_params=pltpu.CompilerParams(
            collective_id=0, has_side_effects=True, vmem_limit_bytes=44 * 1024 * 1024
        ),
        name="darcy_cg",
    )(b, tx, ty, tz, st, perm, kind, count, proj))


def solution(mesh):
    cells = P("sub", "blk", None)
    return jax.shard_map(
        functools.partial(body, mesh), mesh=mesh,
        in_specs=(cells,) * 7 + (P("sub", "blk"), P()), out_specs=(cells, cells), check_vma=False,
    )
```

```python
import functools

import jax
import jax.numpy as jnp
from jax import lax
from jax.experimental import pallas as pl
from jax.experimental.pallas import tpu as pltpu
from jax.sharding import PartitionSpec as P

MESH = pl.DeviceIdType.MESH
F32, BF16, I32 = jnp.float32, jnp.bfloat16, jnp.int32
CX, CY, CZ = 4, 256, 512
FB, KINDS = 128, 4
GROUPS = CZ // FB
NFB = CY * GROUPS
PAD = 8
ROWS = 128
BAND = CY // GROUPS
PENALTY = 4.0


def split(x):
    high = x.astype(BF16)
    low = (x - high.astype(F32)).astype(BF16)
    return jnp.concatenate([high, low], axis=1)


def fold(x):
    total = None
    for r in range(0, x.shape[0], 8):
        for c in range(0, x.shape[1], 128):
            tile = x[r : r + 8, c : c + 128]
            total = tile if total is None else total + tile
    return total


def kernel(n_sub, n_blk, b_hbm, tx_hbm, ty_hbm, tz_hbm, st_hbm, perm_hbm, type_hbm, proj_hbm, count_s,
           B, W, V, scalars,
           TX, TY, TZ, ST,
           perm_v, type_v, meta, meta_in, PROJ,
           wpt, wpp, wm, CB, LOW, NAT, GL, GR, GT,
           face_in, last_in, sl, sl_in, psf, psf_in,
           HL, HL2, HJ, ACC, C2L, J1R, C2R,
           edges, cur, slots,
           load_sem, small_sem, ss, rs, ar_ss, ar_rs):
    s, k = lax.axis_index("sub"), lax.axis_index("blk")
    right, left = (lax.rem(s + 1, n_sub), k), (lax.rem(s + n_sub - 1, n_sub), k)
    up, down = (s, lax.rem(k + 1, n_blk)), (s, lax.rem(k + n_blk - 1, n_blk))
    column = [(lax.rem(s + i, n_sub), k) for i in (10, 6, 14, 9, 11, 2, 5, 7, 13, 8, 3, 4, 12, 1, 15)]
    row = [(s, lax.rem(k + i, n_blk)) for i in (4, 3, 5, 2, 6, 1, 7)]
    near = [column[-2], column[-1], row[-2], row[-1]]
    has_left, has_right, has_down, has_up = s > 0, s < n_sub - 1, k > 0, k < n_blk - 1

    barrier = pltpu.get_barrier_semaphore()
    for peer in near + column[:-2] + row[:-2]:
        pl.semaphore_signal(barrier, inc=1, device_id=peer, device_id_type=MESH)

    small = [
        pltpu.make_async_copy(perm_hbm, perm_v, small_sem.at[0]),
        pltpu.make_async_copy(type_hbm, type_v, small_sem.at[1]),
        pltpu.make_async_copy(proj_hbm, PROJ, small_sem.at[2]),
    ]
    for c in small:
        c.start()

    def load(a, i):
        src, dst = ((b_hbm, B), (tx_hbm, TX), (ty_hbm, TY), (tz_hbm, TZ), (st_hbm, ST))[a]
        to = dst.at[i, pl.ds(PAD, CY), :] if a in (0, 2) else dst.at[i]
        return pltpu.make_async_copy(src.at[i], to, load_sem.at[a, i])

    order = [(0, 3), (0, 2), (2, 3), (3, 3), (4, 3), (1, 2), (0, 0), (0, 1), (2, 0), (3, 0), (4, 0), (1, 0),
             (2, 1), (3, 1), (4, 1), (1, 1), (2, 2), (3, 2), (4, 2)]
    loads = {key: load(*key) for key in order}
    for key in order[:6]:
        loads[key].start()

    @pl.when(s == 0)
    def _():
        meta_in[...] = jnp.zeros_like(meta_in)
        last_in[...] = jnp.zeros_like(last_in)
        sl_in[...] = jnp.zeros_like(sl_in)

    @pl.when(s == n_sub - 1)
    def _():
        face_in[...] = jnp.zeros_like(face_in)
        psf_in[...] = jnp.zeros_like(psf_in)

    @pl.when(k == 0)
    def _():
        for n in (0, 2, 3):
            edges[n] = jnp.zeros((CX, 8, CZ), F32)

    @pl.when(k == n_blk - 1)
    def _():
        for n in (1, 4):
            edges[n] = jnp.zeros((CX, 8, CZ), F32)

    for c in small:
        c.wait()
    meta[0:1, :] = perm_v[0]
    meta[1:2, :] = type_v[0]
    meta[2:3, :] = jnp.full((1, NFB), count_s[0, 0], I32)
    meta[3:8, :] = jnp.zeros((5, NFB), I32)

    pl.semaphore_wait(barrier, n_sub + n_blk - 2)

    class Send:
        def __init__(self, src, dst, n, to, sends, receives):
            self.sends, self.receives = sends, receives
            self.copy = pltpu.make_async_remote_copy(
                src_ref=src, dst_ref=dst, send_sem=ss.at[n], recv_sem=rs.at[n], device_id=to, device_id_type=MESH
            )

        def start(self):
            pl.when(self.sends)(self.copy.start)

        def wait_send(self):
            pl.when(self.sends)(self.copy.wait_send)

        def wait_recv(self):
            pl.when(self.receives)(self.copy.wait_recv)

    to_up, to_down = (up, has_up, has_down), (down, has_down, has_up)
    to_right, to_left = (right, has_right, has_left), (left, has_left, has_right)
    b_up = Send(b_hbm.at[:, CY - 1 : CY, :], edges.at[0, :, 0:1, :], 0, *to_up)
    b_down = Send(b_hbm.at[:, 0:1, :], edges.at[1, :, 0:1, :], 1, *to_down)
    ty_up = Send(ty_hbm.at[:, CY - 1 : CY, :], edges.at[2, :, 0:1, :], 2, *to_up)
    meta_right = Send(meta, meta_in, 3, *to_right)
    w_up = Send(W.at[:, PAD + CY - 1 : PAD + CY, :], edges.at[3, :, 0:1, :], 4, *to_up)
    w_down = Send(W.at[:, PAD : PAD + 1, :], edges.at[4, :, 0:1, :], 5, *to_down)
    quarter = [pl.ds(q * CY, CY) for q in range(GROUPS)]
    sl_right = [Send(sl.at[quarter[q]], sl_in.at[quarter[q]], 6 + q, *to_right) for q in range(GROUPS)]
    psf_left = [Send(psf.at[quarter[q]], psf_in.at[quarter[q]], 10 + q, *to_left) for q in range(GROUPS)]
    parts = [pl.ds(0, CY - BAND), pl.ds(CY - BAND, BAND)]
    first_left = [Send(b_hbm.at[0, p], face_in.at[p], 14 + n, *to_left) for n, p in enumerate(parts)]
    last_right = [Send(b_hbm.at[CX - 1, p], last_in.at[p], 16 + n, *to_right) for n, p in enumerate(parts)]

    b_up.start()
    b_down.start()
    ty_up.start()
    meta_right.start()
    for n in range(2):
        first_left[n].start()
        last_right[n].start()
    for key in order[6:]:
        loads[key].start()

    def place_matrix(target, t, matrix):
        high = matrix.astype(BF16)
        low = (matrix - high.astype(F32)).astype(BF16)
        at, base = slice((t % 2) * FB, (t % 2 + 1) * FB), t // 2
        target[base * 2 * FB : (base * 2 + 1) * FB, at] = high
        target[(base * 2 + 1) * FB : (base * 2 + 2) * FB, at] = high
        target[(4 + base) * FB : (5 + base) * FB, at] = low

    for t in range(KINDS):
        matrix = PROJ[t]
        turned = matrix.T
        place_matrix(wpt, t, turned)
        place_matrix(wpp, t, matrix)
        place_matrix(wm, t, jnp.dot(matrix, turned, precision=lax.Precision.HIGHEST, preferred_element_type=F32))

    lane = lax.broadcasted_iota(I32, (FB, FB), 1)
    sub_row = lax.broadcasted_iota(I32, (FB, FB), 0)

    def columns_of(m, side):
        perm = m[0:1, :]
        y = lax.shift_right_logical(perm, 2)
        place = (lax.shift_right_logical(y, 6) * CY + jnp.bitwise_and(perm, GROUPS - 1) * BAND
                 + jnp.bitwise_and(y, BAND - 1))
        live = (lax.broadcasted_iota(I32, (1, NFB), 1) < m[2:3, :]).astype(I32)
        code = (place + m[1:2, :] * NFB + live * (NFB * KINDS)).astype(F32)
        for i in range(NFB // FB):
            part = jnp.broadcast_to(code[:, i * FB : (i + 1) * FB], (FB, FB))
            NAT[i * FB : (i + 1) * FB, :] = part.T
        for n in range(GROUPS * GROUPS):
            at = slice(n * BAND, (n + 1) * BAND)
            c = NAT[pl.ds((n // GROUPS) * CY + n % GROUPS, BAND, stride=GROUPS), :].astype(I32)
            CB[side, at, :] = c
            LOW[side, at, :] = jnp.where(jnp.bitwise_and(c, 2 * NFB) == 0, 1.0, 0.0).astype(BF16)

    def one_hot(side, G):
        def step(i, _):
            r = pl.multiple_of(i * FB, FB)
            place = jnp.bitwise_and(CB[side, pl.ds(r, FB), :], NFB - 1)
            for j in range(NFB // FB):
                G[pl.ds(r, FB), j * FB : (j + 1) * FB] = jnp.where(place == lane + j * FB, 1.0, 0.0).astype(BF16)
            return 0
        lax.fori_loop(0, NFB // FB, step, 0)

    def one_hot_back(side, G):
        for i in range(NFB // FB):
            place = jnp.bitwise_and(CB[side, i * FB : (i + 1) * FB, :], NFB - 1).astype(F32).T.astype(I32)
            def step(j, _):
                r = pl.multiple_of(j * FB, FB)
                G[pl.ds(r, FB), i * FB : (i + 1) * FB] = jnp.where(place == sub_row + r, 1.0, 0.0).astype(BF16)
                return 0
            lax.fori_loop(0, NFB // FB, step, 0)

    def live_of(side, at):
        return lax.shift_right_logical(CB[side, at, :], 12).astype(F32)

    def pieces(quarters):
        for c in quarters:
            for q in range(GROUPS):
                n = c * GROUPS + q
                yield (slice(n * BAND, (n + 1) * BAND), slice(c * BAND, (c + 1) * BAND), slice(q * FB, (q + 1) * FB),
                       slice(PAD + c * BAND, PAD + (c + 1) * BAND))

    def project(pair, target, side, at=slice(0, NFB)):
        low_kind = LOW[side, at, :]
        high_kind = 1.0 - low_kind
        high, low = pair[:, :FB], pair[:, FB:]
        ha, hb = high * low_kind, high * high_kind
        x = jnp.concatenate([ha, low * low_kind, hb, low * high_kind, ha, hb], axis=1)
        y = jnp.dot(x, target[...], preferred_element_type=F32)
        odd = jnp.bitwise_and(CB[side, at, :], NFB) != 0
        return jnp.where(odd, y[:, FB:], y[:, :FB])

    columns_of(meta, 0)
    one_hot(0, GL)

    def stencil(S, i, c):
        y = pl.multiple_of(c * ROWS, ROWS)
        here, inner = pl.ds(y, ROWS), pl.ds(pl.multiple_of(y + PAD, PAD), ROWS)
        big = S[i, pl.ds(y, ROWS + 2 * PAD), :]
        mid = big[PAD : PAD + ROWS]
        after = pltpu.roll(big, ROWS + 2 * PAD - 1, 0)
        flux = TY[i, pl.ds(y, ROWS + PAD), :] * (big[: PAD + ROWS] - after[: PAD + ROWS])
        out = ST[i, here, :] * mid + (flux[PAD:] - pltpu.roll(flux, 1, 0)[PAD:])
        flux = TZ[i, here, :] * (mid - pltpu.roll(mid, CZ - 1, 1))
        out = out + (flux - pltpu.roll(flux, 1, 1))
        if i < CX - 1:
            out = out + TX[i, here, :] * (mid - S[i + 1, inner, :])
        if i > 0:
            out = out - TX[i - 1, here, :] * (S[i - 1, inner, :] - mid)
        return mid, out, inner, here

    def energy(i, along_x):
        W[i, PAD + CY : PAD + CY + 1, :] = W[i, PAD + CY - 1 : PAD + CY, :]

        def step(c, acc):
            y = pl.multiple_of(c * ROWS, ROWS)
            here, inner = pl.ds(y, ROWS), pl.ds(pl.multiple_of(y + PAD, PAD), ROWS)
            big = W[i, pl.ds(pl.multiple_of(y + PAD, PAD), ROWS + PAD), :]
            mid = big[:ROWS]
            d = mid - pltpu.roll(big, ROWS + PAD - 1, 0)[:ROWS]
            e = ST[i, here, :] * mid * mid + TY[i, inner, :] * d * d
            d = mid - pltpu.roll(mid, CZ - 1, 1)
            e = e + TZ[i, here, :] * d * d
            if along_x:
                d = mid - W[i + 1, inner, :]
                e = e + TX[i, here, :] * d * d
            if i == CX - 1:
                d = W[i - 1, inner, :] - mid
                e = e + TX[i - 1, here, :] * d * d
            return acc + fold(e)

        return lambda acc: lax.fori_loop(0, CY // ROWS, step, acc)

    def prepare(i):
        edge = TZ[i, :, CZ - FB :]
        TZ[i, :, CZ - FB :] = jnp.where(lax.broadcasted_iota(I32, (CY, FB), 1) == FB - 1, 0.0, edge)
        TY[i, PAD + CY - 1 : PAD + CY, :] = jnp.where(has_up, TY[i, PAD + CY - 1 : PAD + CY, :], 0.0)
        TY[i, PAD - 1 : PAD, :] = edges[2, i, 0:1, :]
        B[i, PAD - 1 : PAD, :] = edges[0, i, 0:1, :]
        B[i, PAD + CY : PAD + CY + 1, :] = edges[1, i, 0:1, :]

    for a, i in order[:6]:
        loads[a, i].wait()
    b_up.wait_recv()
    b_down.wait_recv()
    ty_up.wait_recv()
    prepare(3)

    def last_face(c, _):
        mid, out, inner, here = stencil(B, 3, c)
        W[3, inner, :] = out
        for n in range(ROWS // BAND * GROUPS):
            h, q = divmod(n, GROUPS)
            at = pl.ds(pl.multiple_of(c * (ROWS * GROUPS) + n * BAND, BAND), BAND)
            sl[at, :] = out[h * BAND : (h + 1) * BAND, q * FB : (q + 1) * FB]
        return 0

    lax.fori_loop(0, CY // ROWS, last_face, 0)
    for q in (2, 3, 0, 1):
        sl_right[q].start()

    for a, i in order[6:12]:
        loads[a, i].wait()
    prepare(0)

    def first_face(c, _):
        mid, out, inner, here = stencil(B, 0, c)
        W[0, inner, :] = out
        for n in range(ROWS // BAND * GROUPS):
            h, q = divmod(n, GROUPS)
            at = pl.ds(pl.multiple_of(c * (ROWS * GROUPS) + n * BAND, BAND), BAND)
            ys, cols = slice(h * BAND, (h + 1) * BAND), slice(q * FB, (q + 1) * FB)
            HL[at, :] = split(mid[ys, cols])
            HL2[at, :] = split(out[ys, cols])
        return 0

    lax.fori_loop(0, CY // ROWS, first_face, 0)

    meta_right.wait_recv()
    columns_of(meta_in, 1)
    one_hot(1, GR)
    g = jnp.dot(GR[...], HL2[...], preferred_element_type=F32).astype(BF16)
    psf[...] = project(g, wpt, 1)
    for q in range(GROUPS):
        psf_left[q].start()
    g = jnp.dot(GR[...], HL[...], preferred_element_type=F32).astype(BF16)
    J1R[...] = project(g, wpt, 1)

    one_hot_back(1, GT)

    for a, i in order[12:]:
        loads[a, i].wait()
    zero = jnp.zeros((8, 128), F32)
    sums = (zero, zero, zero)
    for i in (1, 2):
        prepare(i)

        def middle(c, acc, i=i):
            mid, out, inner, here = stencil(B, i, c)
            W[i, inner, :] = out
            return acc[0] + fold(mid * mid), acc[1] + fold(mid * out), acc[2] + fold(out * out)

        sums = lax.fori_loop(0, CY // ROWS, middle, sums)
    wv = energy(1, True)(zero)
    wv = energy(2, False)(wv)

    right_one, left_one = has_right.astype(F32), has_left.astype(F32)
    most, rest = slice(0, NFB - CY), slice(NFB - CY, NFB)

    def gather_right(quarters, at):
        for rows, ys, cols, _ in pieces(quarters):
            HL[rows, :] = split(face_in[ys, cols])
        return jnp.dot(GL[:, at], HL[at, :], preferred_element_type=F32)

    def jumps_left(quarters, at):
        for rows, ys, cols, _ in pieces(quarters):
            jump = left_one * live_of(1, rows) * (last_in[ys, cols] - J1R[rows, :])
            HJ[rows, :] = split(jump)
            C2R[rows, :] = PENALTY * jump - psf[rows, :]
        HL2[at, :] = split(project(HJ[at, :], wpp, 1, at))
        return jnp.dot(GT[:, at], HL2[at, :], preferred_element_type=F32)

    first_left[0].wait_recv()
    last_right[0].wait_recv()
    ACC[...] = gather_right((0, 1, 2), most)
    g = jumps_left((0, 1, 2), most)
    for at, _, cols, ys in pieces(range(GROUPS)):
        W[0, ys, cols] = W[0, ys, cols] - PENALTY * (g[at, :FB] + g[at, FB:])
    first_left[1].wait_recv()
    last_right[1].wait_recv()
    g = jumps_left((3,), rest)
    for at, _, cols, ys in pieces(range(GROUPS)):
        w = W[0, ys, cols] - PENALTY * (g[at, :FB] + g[at, FB:])
        W[0, ys, cols] = w
        mid = B[0, ys, cols]
        sums = sums[0] + fold(mid * mid), sums[1] + fold(mid * w), sums[2] + fold(w * w)
    g = ACC[...] + gather_right((3,), rest)
    projected = project(g.astype(BF16), wpt, 0)
    for at, _, cols, ys in pieces(range(GROUPS)):
        mid = B[3, ys, cols]
        jump = live_of(0, at) * (mid - projected[at])
        w = W[3, ys, cols] + PENALTY * jump
        W[3, ys, cols] = w
        HL[at, :] = split(jump)
        C2L[at, :] = w
        sums = sums[0] + fold(mid * mid), sums[1] + fold(mid * w), sums[2] + fold(w * w)

    w_up.start()
    w_down.start()

    C2L[...] = C2L[...] + (PENALTY * right_one) * project(HL[...], wm, 0)
    C2R[...] = C2R[...] + PENALTY * project(HJ[...], wm, 1)
    wv = energy(0, True)(wv)
    wv = energy(3, False)(wv)

    def left_jump(q, wait=True):
        at = slice(q * CY, (q + 1) * CY)
        if wait:
            psf_left[q].wait_recv()
        return live_of(0, at) * (C2L[at, :] - psf_in[at, :])

    def right_jump(q):
        at = slice(q * CY, (q + 1) * CY)
        sl_right[q].wait_recv()
        return left_one * live_of(1, at) * (sl_in[at, :] + C2R[at, :])

    def add_left(q, jump):
        for at, ys, cols, _ in pieces((q,)):
            V[3, ys, cols] = V[3, ys, cols] + PENALTY * jump[at.start - q * CY : at.stop - q * CY]

    def add_right(pair, at):
        back = split(project(pair, wpp, 1, at))
        g = jnp.dot(GT[:, at], back, preferred_element_type=F32)
        for rows, ys, cols, _ in pieces(range(GROUPS)):
            V[0, ys, cols] = V[0, ys, cols] - PENALTY * (g[rows, :FB] + g[rows, FB:])

    no_right = 1.0 - right_one
    mortar = zero
    for q in (2, 3):
        at = slice(q * CY, (q + 1) * CY)
        only = live_of(0, at) * C2L[at, :]
        mortar = mortar + no_right * fold(only * only)
    for q in (0, 1):
        jump = left_jump(q)
        mortar = mortar + fold(jump * jump)
    for q in (2, 3):
        jump = right_jump(q)
        HJ[q * CY : (q + 1) * CY, :] = split(jump)
        mortar = mortar + fold(jump * jump)
    wv = wv + PENALTY * mortar

    w_up.wait_recv()
    w_down.wait_recv()
    across = jnp.zeros((1, CZ), F32)
    for i in range(CX):
        d = W[i, PAD + CY - 1 : PAD + CY, :] - edges[4, i, 0:1, :]
        across = across + TY[i, PAD + CY - 1 : PAD + CY, :] * d * d
        W[i, PAD - 1 : PAD, :] = edges[3, i, 0:1, :]
        W[i, PAD + CY : PAD + CY + 1, :] = edges[4, i, 0:1, :]

    lane_row = lax.broadcasted_iota(I32, (1, 128), 1)
    packed = jnp.zeros((1, 128), F32)
    for n, part in enumerate((sums[0], sums[1], sums[2])):
        packed = jnp.where(lane_row == n, jnp.sum(part), packed)
    packed = jnp.where(lane_row == 3, jnp.sum(wv) + jnp.sum(across), packed)
    cur[0, 0:1, :] = packed

    def spread(stage, peers):
        for i, peer in enumerate(peers):
            pltpu.make_async_remote_copy(
                src_ref=cur.at[stage, 0:1], dst_ref=slots.at[stage, i : i + 1],
                send_sem=ar_ss.at[stage], recv_sem=ar_rs.at[stage], device_id=peer, device_id_type=MESH,
            ).start()
        return len(peers)

    def collect(stage, count):
        arrived = slots.at[stage, 0:count]
        pltpu.make_async_copy(arrived, arrived, ar_rs.at[stage]).wait()
        return cur[stage, 0:1, :] + jnp.sum(slots[stage, 0:count, :], axis=0, keepdims=True)

    n0 = spread(0, column)

    for i in (3, 0, 1, 2):
        def second(c, _, i=i):
            mid, out, inner, here = stencil(W, i, c)
            V[i, here, :] = out
            return 0
        lax.fori_loop(0, CY // ROWS, second, 0)
    for q in (0, 1):
        add_left(q, left_jump(q, wait=False))
    add_right(HJ[2 * CY :, :], slice(2 * CY, 4 * CY))

    cur[1, 0:1, :] = collect(0, n0)
    n1 = spread(1, row)

    for q in (2, 3):
        add_left(q, left_jump(q))
    for q in (0, 1):
        add_right(split(right_jump(q)), slice(q * CY, (q + 1) * CY))

    total = collect(1, n1)
    bb, bw, ww, wv = (total[0:1, n : n + 1] for n in range(4))
    alpha = bb / bw
    rr = alpha * alpha * ww - bb
    beta = rr / bb
    curve = bw - 2.0 * alpha * ww + alpha * alpha * wv - beta * beta * bw
    alpha2 = rr / curve
    scalars[0:8, :] = jnp.broadcast_to(alpha + alpha2 * (1.0 + beta), (8, 128))
    scalars[8:16, :] = jnp.broadcast_to(alpha * alpha2, (8, 128))

    for c in [b_up, b_down, ty_up, meta_right, w_up, w_down] + first_left + last_right + sl_right + psf_left:
        c.wait_send()
    for stage, count in ((0, n0), (1, n1)):
        sent = slots.at[stage, 0:count]
        pltpu.make_async_copy(sent, sent, ar_ss.at[stage]).wait()


def finish_kernel(B, W, V, scalars, x_hbm, r_hbm, x_v, r_v, sem):
    first, cross = scalars[0:1, 0:1], scalars[8:9, 0:1]
    out = []
    for i in range(CX):
        for h in range(2):
            n = 2 * i + h
            here, inner = pl.ds(h * ROWS, ROWS), pl.ds(PAD + h * ROWS, ROWS)
            b, w = B[i, inner, :], W[i, inner, :]
            x_v[i, here, :] = first * b - cross * w
            out.append(pltpu.make_async_copy(x_v.at[i, here], x_hbm.at[i, here], sem.at[0, n]))
            out[-1].start()
            r_v[i, here, :] = b - first * w + cross * V[i, here, :]
            out.append(pltpu.make_async_copy(r_v.at[i, here], r_hbm.at[i, here], sem.at[1, n]))
            out[-1].start()
    for c in out:
        c.wait()


def body(mesh, b, tx, ty, tz, st, perm, kind, count, proj):
    n_sub, n_blk = mesh.shape["sub"], mesh.shape["blk"]
    vm = lambda *shape, dtype=F32: pltpu.VMEM(shape, dtype)
    face, block, padded = (NFB, FB), (CX, CY, CZ), (CX, CY + 2 * PAD, CZ)
    scratch = [
        vm(*block), vm(CX, CY + PAD, CZ), vm(*block), vm(*block),
        vm(1, 1, NFB, dtype=I32), vm(1, 1, NFB, dtype=I32),
        vm(8, NFB, dtype=I32), vm(8, NFB, dtype=I32), vm(KINDS, FB, FB),
        vm(6 * FB, 2 * FB, dtype=BF16), vm(6 * FB, 2 * FB, dtype=BF16), vm(6 * FB, 2 * FB, dtype=BF16),
        vm(2, NFB, FB, dtype=I32), vm(2, NFB, FB, dtype=BF16), vm(*face),
        vm(NFB, NFB, dtype=BF16), vm(NFB, NFB, dtype=BF16), vm(NFB, NFB, dtype=BF16),
        vm(CY, CZ), vm(CY, CZ), vm(*face), vm(*face), vm(*face), vm(*face),
        vm(NFB, 2 * FB, dtype=BF16), vm(NFB, 2 * FB, dtype=BF16), vm(NFB, 2 * FB, dtype=BF16), vm(NFB, 2 * FB),
        vm(*face), vm(*face), vm(*face),
        vm(5, CX, 8, CZ), vm(2, 8, 128), vm(2, 16, 128),
        pltpu.SemaphoreType.DMA((5, CX)), pltpu.SemaphoreType.DMA((3,)),
        pltpu.SemaphoreType.DMA((18,)), pltpu.SemaphoreType.DMA((18,)),
        pltpu.SemaphoreType.DMA((2,)), pltpu.SemaphoreType.DMA((2,)),
    ]
    like = lambda *shape: jax.ShapeDtypeStruct(shape, F32)
    in_vmem, in_hbm = pl.BlockSpec(memory_space=pltpu.VMEM), pl.BlockSpec(memory_space=pltpu.HBM)
    args = [pltpu.with_memory_space_constraint(a, pltpu.HBM) for a in (b, tx, ty, tz, st, perm, kind, proj)]
    state = pl.pallas_call(
        functools.partial(kernel, n_sub, n_blk),
        out_shape=(vm(*padded), vm(*padded), vm(*block), vm(16, 128)),
        in_specs=[in_hbm] * 8 + [pl.BlockSpec(memory_space=pltpu.SMEM)],
        out_specs=(in_vmem,) * 4,
        scratch_shapes=scratch,
        compiler_params=pltpu.CompilerParams(
            collective_id=0, has_side_effects=True, vmem_limit_bytes=48 * 1024 * 1024
        ),
        name="darcy_cg",
    )(*args, count)
    return tuple(pl.pallas_call(
        finish_kernel,
        out_shape=(like(*block), like(*block)),
        in_specs=[in_vmem] * 4,
        out_specs=(in_hbm,) * 2,
        scratch_shapes=[vm(*block), vm(*block), pltpu.SemaphoreType.DMA((2, 2 * CX))],
        compiler_params=pltpu.CompilerParams(vmem_limit_bytes=32 * 1024 * 1024),
        name="finish",
    )(*state))


def solution(mesh):
    cells = P("sub", "blk", None)
    return jax.shard_map(
        functools.partial(body, mesh), mesh=mesh,
        in_specs=(cells,) * 7 + (P("sub", "blk"), P()), out_specs=(cells, cells), check_vma=False,
    )
```

```python
import functools

import jax
import jax.numpy as jnp
from jax import lax
from jax.experimental import pallas as pl
from jax.experimental.pallas import tpu as pltpu
from jax.sharding import PartitionSpec as P

MESH = pl.DeviceIdType.MESH
F32, BF16, I32 = jnp.float32, jnp.bfloat16, jnp.int32
CX, CY, CZ = 4, 256, 512
FB, KINDS = 128, 4
GROUPS = CZ // FB
NFB = CY * GROUPS
PAD = 8
ROWS = 128
BAND = CY // GROUPS
PENALTY = 4.0


def split(x):
    high = x.astype(BF16)
    low = (x - high.astype(F32)).astype(BF16)
    return jnp.concatenate([high, low], axis=1)


def fold(x):
    total = None
    for r in range(0, x.shape[0], 8):
        for c in range(0, x.shape[1], 128):
            tile = x[r : r + 8, c : c + 128]
            total = tile if total is None else total + tile
    return total


def kernel(n_sub, n_blk, b_hbm, tx_hbm, ty_hbm, tz_hbm, st_hbm, perm_hbm, type_hbm, proj_hbm, count_s,
           B, W, V, scalars,
           TX, TY, TZ, ST,
           perm_v, type_v, count_v, perm_in, type_in, count_in, PROJ,
           wpt, wpp, wm, CB, LOW, NAT, GL, GR, GT,
           face_in, last_in, sl, sl_in, psf, psf_in,
           HL, HL2, HJ, ACC, C2L, J1R, C2R,
           edges, cur, slots, known,
           load_sem, small_sem, ss, rs, ar_ss, ar_rs):
    s, k = lax.axis_index("sub"), lax.axis_index("blk")
    right, left = (lax.rem(s + 1, n_sub), k), (lax.rem(s + n_sub - 1, n_sub), k)
    up, down = (s, lax.rem(k + 1, n_blk)), (s, lax.rem(k + n_blk - 1, n_blk))
    column = [(lax.rem(s + i, n_sub), k) for i in (10, 6, 14, 9, 11, 2, 5, 7, 13, 8, 3, 4, 12, 1, 15)]
    row = [(s, lax.rem(k + i, n_blk)) for i in (4, 3, 5, 2, 6, 1, 7)]
    has_left, has_right, has_down, has_up = s > 0, s < n_sub - 1, k > 0, k < n_blk - 1

    def along(axis, distance):
        for step in (distance, -distance):
            here, size = (s, n_sub) if axis == "sub" else (k, n_blk)
            exists = here + step < size if step > 0 else here + step >= 0
            yield exists, ((s + step, k) if axis == "sub" else (s, k + step))

    def tell(axis, distance, semaphore):
        for exists, peer in along(axis, distance):
            @pl.when(exists)
            def _():
                pl.semaphore_signal(semaphore, inc=1, device_id=peer, device_id_type=MESH)

    def hear(axis, distance, semaphore):
        pl.semaphore_wait(semaphore, sum(exists.astype(I32) for exists, _ in along(axis, distance)))

    barrier = pltpu.get_barrier_semaphore()
    tell("sub", 1, barrier)
    tell("blk", 1, barrier)

    small = [
        pltpu.make_async_copy(perm_hbm, perm_v, small_sem.at[0]),
        pltpu.make_async_copy(type_hbm, type_v, small_sem.at[1]),
        pltpu.make_async_copy(proj_hbm, PROJ, small_sem.at[2]),
    ]
    for c in small:
        c.start()

    def load(a, i):
        src, dst = ((b_hbm, B), (tx_hbm, TX), (ty_hbm, TY), (tz_hbm, TZ), (st_hbm, ST))[a]
        to = dst.at[i, pl.ds(PAD, CY), :] if a in (0, 2) else dst.at[i]
        return pltpu.make_async_copy(src.at[i], to, load_sem.at[a, i])

    order = [(0, 3), (0, 2), (2, 3), (3, 3), (4, 3), (1, 2), (0, 0), (0, 1), (2, 0), (3, 0), (4, 0), (1, 0),
             (2, 1), (3, 1), (4, 1), (1, 1), (2, 2), (3, 2), (4, 2)]
    loads = {key: load(*key) for key in order}
    for key in order[:6]:
        loads[key].start()

    @pl.when(s == 0)
    def _():
        for ref in (perm_in, type_in, count_in):
            ref[...] = jnp.zeros_like(ref)
        last_in[...] = jnp.zeros_like(last_in)
        sl_in[...] = jnp.zeros_like(sl_in)

    @pl.when(s == n_sub - 1)
    def _():
        face_in[...] = jnp.zeros_like(face_in)
        psf_in[...] = jnp.zeros_like(psf_in)

    @pl.when(k == 0)
    def _():
        for n in (0, 2, 3):
            edges[n] = jnp.zeros((CX, 8, CZ), F32)

    @pl.when(k == n_blk - 1)
    def _():
        for n in (1, 4):
            edges[n] = jnp.zeros((CX, 8, CZ), F32)

    count_v[...] = jnp.full((8, FB), count_s[0, 0], I32)

    pl.semaphore_wait(barrier, sum(e.astype(I32) for e in (has_left, has_right, has_down, has_up)))

    class Send:
        def __init__(self, src, dst, n, to, sends, receives):
            self.sends, self.receives = sends, receives
            self.copy = pltpu.make_async_remote_copy(
                src_ref=src, dst_ref=dst, send_sem=ss.at[n], recv_sem=rs.at[n], device_id=to, device_id_type=MESH
            )

        def start(self):
            pl.when(self.sends)(self.copy.start)

        def wait_send(self):
            pl.when(self.sends)(self.copy.wait_send)

        def wait_recv(self):
            pl.when(self.receives)(self.copy.wait_recv)

    to_up, to_down = (up, has_up, has_down), (down, has_down, has_up)
    to_right, to_left = (right, has_right, has_left), (left, has_left, has_right)
    pairs_right = [Send(perm_hbm, perm_in, 0, *to_right), Send(type_hbm, type_in, 1, *to_right),
                   Send(count_v, count_in, 2, *to_right)]
    b_up = Send(b_hbm.at[:, CY - 1 : CY, :], edges.at[0, :, 0:1, :], 3, *to_up)
    b_down = Send(b_hbm.at[:, 0:1, :], edges.at[1, :, 0:1, :], 4, *to_down)
    ty_up = Send(ty_hbm.at[:, CY - 1 : CY, :], edges.at[2, :, 0:1, :], 5, *to_up)

    def w_edges(at, n):
        return [Send(W.at[at, PAD + CY - 1 : PAD + CY, :], edges.at[3, at, 0:1, :], n, *to_up),
                Send(W.at[at, PAD : PAD + 1, :], edges.at[4, at, 0:1, :], n + 1, *to_down)]

    w_inner, w_first, w_last = w_edges(pl.ds(1, 2), 6), w_edges(pl.ds(0, 1), 8), w_edges(pl.ds(3, 1), 10)
    quarter = [pl.ds(q * CY, CY) for q in range(GROUPS)]
    sl_right = [Send(sl.at[quarter[q]], sl_in.at[quarter[q]], 12 + q, *to_right) for q in range(GROUPS)]
    psf_left = [Send(psf.at[quarter[q]], psf_in.at[quarter[q]], 16 + q, *to_left) for q in range(GROUPS)]
    parts = [pl.ds(0, CY - BAND), pl.ds(CY - BAND, BAND)]
    first_left = [Send(b_hbm.at[0, p], face_in.at[p], 20 + n, *to_left) for n, p in enumerate(parts)]
    last_right = [Send(b_hbm.at[CX - 1, p], last_in.at[p], 22 + n, *to_right) for n, p in enumerate(parts)]

    for c in pairs_right:
        c.start()
    for n in range(2):
        first_left[n].start()
        last_right[n].start()
    b_up.start()
    b_down.start()
    ty_up.start()
    tell("sub", 1, known.at[0])
    tell("blk", 1, known.at[4])
    for key in order[6:]:
        loads[key].start()
    for c in small:
        c.wait()

    def place_matrix(target, t, matrix):
        high = matrix.astype(BF16)
        low = (matrix - high.astype(F32)).astype(BF16)
        at, base = slice((t % 2) * FB, (t % 2 + 1) * FB), t // 2
        target[base * 2 * FB : (base * 2 + 1) * FB, at] = high
        target[(base * 2 + 1) * FB : (base * 2 + 2) * FB, at] = high
        target[(4 + base) * FB : (5 + base) * FB, at] = low

    for t in range(KINDS):
        matrix = PROJ[t]
        turned = matrix.T
        place_matrix(wpt, t, turned)
        place_matrix(wpp, t, matrix)
        place_matrix(wm, t, jnp.dot(matrix, turned, precision=lax.Precision.HIGHEST, preferred_element_type=F32))

    lane = lax.broadcasted_iota(I32, (FB, FB), 1)
    sub_row = lax.broadcasted_iota(I32, (FB, FB), 0)

    def columns_of(perm_ref, type_ref, count_ref, side):
        for i in range(NFB // FB):
            at = slice(i * FB, (i + 1) * FB)
            perm = perm_ref[0, :, at]
            y = lax.shift_right_logical(perm, 2)
            place = (lax.shift_right_logical(y, 6) * CY + jnp.bitwise_and(perm, GROUPS - 1) * BAND
                     + jnp.bitwise_and(y, BAND - 1))
            live = (lax.broadcasted_iota(I32, (1, FB), 1) + i * FB < count_ref[0:1, :]).astype(I32)
            code = (place + type_ref[0, :, at] * NFB + live * (NFB * KINDS)).astype(F32)
            NAT[at, :] = jnp.broadcast_to(code, (FB, FB)).T
        for n in range(GROUPS * GROUPS):
            at = slice(n * BAND, (n + 1) * BAND)
            c = NAT[pl.ds((n // GROUPS) * CY + n % GROUPS, BAND, stride=GROUPS), :].astype(I32)
            CB[side, at, :] = c
            LOW[side, at, :] = jnp.where(jnp.bitwise_and(c, 2 * NFB) == 0, 1.0, 0.0).astype(BF16)

    def one_hot(side, G):
        def step(i, _):
            r = pl.multiple_of(i * FB, FB)
            place = jnp.bitwise_and(CB[side, pl.ds(r, FB), :], NFB - 1)
            for j in range(NFB // FB):
                G[pl.ds(r, FB), j * FB : (j + 1) * FB] = jnp.where(place == lane + j * FB, 1.0, 0.0).astype(BF16)
            return 0
        lax.fori_loop(0, NFB // FB, step, 0)

    def one_hot_back(side, G):
        for i in range(NFB // FB):
            place = jnp.bitwise_and(CB[side, i * FB : (i + 1) * FB, :], NFB - 1).astype(F32).T.astype(I32)
            def step(j, _):
                r = pl.multiple_of(j * FB, FB)
                G[pl.ds(r, FB), i * FB : (i + 1) * FB] = jnp.where(place == sub_row + r, 1.0, 0.0).astype(BF16)
                return 0
            lax.fori_loop(0, NFB // FB, step, 0)

    def live_of(side, at):
        return lax.shift_right_logical(CB[side, at, :], 12).astype(F32)

    def pieces(quarters):
        for c in quarters:
            for q in range(GROUPS):
                n = c * GROUPS + q
                yield (slice(n * BAND, (n + 1) * BAND), slice(c * BAND, (c + 1) * BAND), slice(q * FB, (q + 1) * FB),
                       slice(PAD + c * BAND, PAD + (c + 1) * BAND))

    def project(pair, target, side, at=slice(0, NFB)):
        low_kind = LOW[side, at, :]
        high_kind = 1.0 - low_kind
        high, low = pair[:, :FB], pair[:, FB:]
        ha, hb = high * low_kind, high * high_kind
        x = jnp.concatenate([ha, low * low_kind, hb, low * high_kind, ha, hb], axis=1)
        y = jnp.dot(x, target[...], preferred_element_type=F32)
        odd = jnp.bitwise_and(CB[side, at, :], NFB) != 0
        return jnp.where(odd, y[:, FB:], y[:, :FB])

    columns_of(perm_v, type_v, count_v, 0)
    one_hot(0, GL)

    def stencil(S, i, c):
        y = pl.multiple_of(c * ROWS, ROWS)
        here, inner = pl.ds(y, ROWS), pl.ds(pl.multiple_of(y + PAD, PAD), ROWS)
        big = S[i, pl.ds(y, ROWS + 2 * PAD), :]
        mid = big[PAD : PAD + ROWS]
        after = pltpu.roll(big, ROWS + 2 * PAD - 1, 0)
        flux = TY[i, pl.ds(y, ROWS + PAD), :] * (big[: PAD + ROWS] - after[: PAD + ROWS])
        out = ST[i, here, :] * mid + (flux[PAD:] - pltpu.roll(flux, 1, 0)[PAD:])
        flux = TZ[i, here, :] * (mid - pltpu.roll(mid, CZ - 1, 1))
        out = out + (flux - pltpu.roll(flux, 1, 1))
        if i < CX - 1:
            out = out + TX[i, here, :] * (mid - S[i + 1, inner, :])
        if i > 0:
            out = out - TX[i - 1, here, :] * (S[i - 1, inner, :] - mid)
        return mid, out, inner, here

    def energy(i, along_x):
        W[i, PAD + CY : PAD + CY + 1, :] = W[i, PAD + CY - 1 : PAD + CY, :]

        def step(c, acc):
            y = pl.multiple_of(c * ROWS, ROWS)
            here, inner = pl.ds(y, ROWS), pl.ds(pl.multiple_of(y + PAD, PAD), ROWS)
            big = W[i, pl.ds(pl.multiple_of(y + PAD, PAD), ROWS + PAD), :]
            mid = big[:ROWS]
            d = mid - pltpu.roll(big, ROWS + PAD - 1, 0)[:ROWS]
            e = ST[i, here, :] * mid * mid + TY[i, inner, :] * d * d
            d = mid - pltpu.roll(mid, CZ - 1, 1)
            e = e + TZ[i, here, :] * d * d
            if along_x:
                d = mid - W[i + 1, inner, :]
                e = e + TX[i, here, :] * d * d
            if i == CX - 1:
                d = W[i - 1, inner, :] - mid
                e = e + TX[i - 1, here, :] * d * d
            return acc + fold(e)

        return lambda acc: lax.fori_loop(0, CY // ROWS, step, acc)

    def prepare(i):
        edge = TZ[i, :, CZ - FB :]
        TZ[i, :, CZ - FB :] = jnp.where(lax.broadcasted_iota(I32, (CY, FB), 1) == FB - 1, 0.0, edge)
        TY[i, PAD + CY - 1 : PAD + CY, :] = jnp.where(has_up, TY[i, PAD + CY - 1 : PAD + CY, :], 0.0)
        TY[i, PAD - 1 : PAD, :] = edges[2, i, 0:1, :]
        B[i, PAD - 1 : PAD, :] = edges[0, i, 0:1, :]
        B[i, PAD + CY : PAD + CY + 1, :] = edges[1, i, 0:1, :]

    for a, i in order[:6]:
        loads[a, i].wait()
    b_up.wait_recv()
    b_down.wait_recv()
    ty_up.wait_recv()
    prepare(3)

    def last_face(c, _):
        mid, out, inner, here = stencil(B, 3, c)
        W[3, inner, :] = out
        for n in range(ROWS // BAND * GROUPS):
            h, q = divmod(n, GROUPS)
            at = pl.ds(pl.multiple_of(c * (ROWS * GROUPS) + n * BAND, BAND), BAND)
            sl[at, :] = out[h * BAND : (h + 1) * BAND, q * FB : (q + 1) * FB]
        return 0

    lax.fori_loop(0, CY // ROWS, last_face, 0)
    for q in (2, 3, 0, 1):
        sl_right[q].start()

    hear("sub", 1, known.at[0])
    tell("sub", 2, known.at[1])
    hear("blk", 1, known.at[4])
    tell("blk", 2, known.at[5])

    for a, i in order[6:12]:
        loads[a, i].wait()
    prepare(0)

    def first_face(c, _):
        mid, out, inner, here = stencil(B, 0, c)
        W[0, inner, :] = out
        for n in range(ROWS // BAND * GROUPS):
            h, q = divmod(n, GROUPS)
            at = pl.ds(pl.multiple_of(c * (ROWS * GROUPS) + n * BAND, BAND), BAND)
            ys, cols = slice(h * BAND, (h + 1) * BAND), slice(q * FB, (q + 1) * FB)
            HL[at, :] = split(mid[ys, cols])
            HL2[at, :] = split(out[ys, cols])
        return 0

    lax.fori_loop(0, CY // ROWS, first_face, 0)

    for c in pairs_right:
        c.wait_recv()
    columns_of(perm_in, type_in, count_in, 1)
    one_hot(1, GR)
    g = jnp.dot(GR[...], HL2[...], preferred_element_type=F32).astype(BF16)
    psf[...] = project(g, wpt, 1)
    for q in range(GROUPS):
        psf_left[q].start()
    hear("sub", 2, known.at[1])
    tell("sub", 4, known.at[2])
    hear("blk", 2, known.at[5])
    tell("blk", 4, known.at[6])
    g = jnp.dot(GR[...], HL[...], preferred_element_type=F32).astype(BF16)
    J1R[...] = project(g, wpt, 1)

    one_hot_back(1, GT)

    for a, i in order[12:]:
        loads[a, i].wait()
    zero = jnp.zeros((8, 128), F32)
    sums = (zero, zero, zero)
    for i in (1, 2):
        prepare(i)

        def middle(c, acc, i=i):
            mid, out, inner, here = stencil(B, i, c)
            W[i, inner, :] = out
            return acc[0] + fold(mid * mid), acc[1] + fold(mid * out), acc[2] + fold(out * out)

        sums = lax.fori_loop(0, CY // ROWS, middle, sums)
    for c in w_inner:
        c.start()
    hear("sub", 4, known.at[2])
    tell("sub", 8, known.at[3])
    hear("blk", 4, known.at[6])
    wv = energy(1, True)(zero)
    wv = energy(2, False)(wv)

    right_one, left_one = has_right.astype(F32), has_left.astype(F32)
    most, rest = slice(0, NFB - CY), slice(NFB - CY, NFB)

    def gather_right(quarters, at):
        for rows, ys, cols, _ in pieces(quarters):
            HL[rows, :] = split(face_in[ys, cols])
        return jnp.dot(GL[:, at], HL[at, :], preferred_element_type=F32)

    def jumps_left(quarters, at):
        for rows, ys, cols, _ in pieces(quarters):
            jump = left_one * live_of(1, rows) * (last_in[ys, cols] - J1R[rows, :])
            HJ[rows, :] = split(jump)
            C2R[rows, :] = PENALTY * jump - psf[rows, :]
        HL2[at, :] = split(project(HJ[at, :], wpp, 1, at))
        return jnp.dot(GT[:, at], HL2[at, :], preferred_element_type=F32)

    first_left[0].wait_recv()
    last_right[0].wait_recv()
    ACC[...] = gather_right((0, 1, 2), most)
    g = jumps_left((0, 1, 2), most)
    for at, _, cols, ys in pieces(range(GROUPS)):
        W[0, ys, cols] = W[0, ys, cols] - PENALTY * (g[at, :FB] + g[at, FB:])
    first_left[1].wait_recv()
    last_right[1].wait_recv()
    g = jumps_left((3,), rest)
    for at, _, cols, ys in pieces(range(GROUPS)):
        w = W[0, ys, cols] - PENALTY * (g[at, :FB] + g[at, FB:])
        W[0, ys, cols] = w
        mid = B[0, ys, cols]
        sums = sums[0] + fold(mid * mid), sums[1] + fold(mid * w), sums[2] + fold(w * w)
    for c in w_first:
        c.start()
    g = ACC[...] + gather_right((3,), rest)
    projected = project(g.astype(BF16), wpt, 0)
    for at, _, cols, ys in pieces(range(GROUPS)):
        mid = B[3, ys, cols]
        jump = live_of(0, at) * (mid - projected[at])
        w = W[3, ys, cols] + PENALTY * jump
        W[3, ys, cols] = w
        HL[at, :] = split(jump)
        C2L[at, :] = w
        sums = sums[0] + fold(mid * mid), sums[1] + fold(mid * w), sums[2] + fold(w * w)

    for c in w_last:
        c.start()

    C2L[...] = C2L[...] + (PENALTY * right_one) * project(HL[...], wm, 0)
    C2R[...] = C2R[...] + PENALTY * project(HJ[...], wm, 1)
    wv = energy(0, True)(wv)
    wv = energy(3, False)(wv)

    def left_jump(q, wait=True):
        at = slice(q * CY, (q + 1) * CY)
        if wait:
            psf_left[q].wait_recv()
        return live_of(0, at) * (C2L[at, :] - psf_in[at, :])

    def right_jump(q, wait=True):
        at = slice(q * CY, (q + 1) * CY)
        if wait:
            sl_right[q].wait_recv()
        return left_one * live_of(1, at) * (sl_in[at, :] + C2R[at, :])

    def add_left(q, jump):
        for at, ys, cols, _ in pieces((q,)):
            V[3, ys, cols] = V[3, ys, cols] + PENALTY * jump[at.start - q * CY : at.stop - q * CY]

    def add_right(pair, at):
        back = split(project(pair, wpp, 1, at))
        g = jnp.dot(GT[:, at], back, preferred_element_type=F32)
        for rows, ys, cols, _ in pieces(range(GROUPS)):
            V[0, ys, cols] = V[0, ys, cols] - PENALTY * (g[rows, :FB] + g[rows, FB:])

    mortar = zero
    for q in (2, 3):
        at = slice(q * CY, (q + 1) * CY)
        only = live_of(0, at) * C2L[at, :]
        mortar = mortar + (1.0 - right_one) * fold(only * only)
    hear("sub", 8, known.at[3])
    for c in w_inner + w_first + w_last:
        c.wait_recv()
    across = jnp.zeros((1, CZ), F32)
    for i in range(CX):
        d = W[i, PAD + CY - 1 : PAD + CY, :] - edges[4, i, 0:1, :]
        across = across + TY[i, PAD + CY - 1 : PAD + CY, :] * d * d
        W[i, PAD - 1 : PAD, :] = edges[3, i, 0:1, :]
        W[i, PAD + CY : PAD + CY + 1, :] = edges[4, i, 0:1, :]
    lane_row = lax.broadcasted_iota(I32, (1, FB), 1)
    packed = jnp.zeros((1, FB), F32)
    for n, part in enumerate(sums):
        packed = jnp.where(lane_row == n, jnp.sum(part), packed)
    packed = jnp.where(lane_row == 3, jnp.sum(wv) + jnp.sum(across), packed)
    for n in range(2):
        jump = left_jump(n)
        mortar = mortar + fold(jump * jump)
        jump = right_jump(2 + n)
        mortar = mortar + fold(jump * jump)

    def spread(stage, part, peers):
        cur[stage, 0:1, :] = part
        for n, peer in enumerate(peers):
            pltpu.make_async_remote_copy(
                src_ref=cur.at[stage, 0:1], dst_ref=slots.at[stage, n : n + 1],
                send_sem=ar_ss.at[stage], recv_sem=ar_rs.at[stage], device_id=peer, device_id_type=MESH,
            ).start()

    def collect(stage, peers):
        arrived = slots.at[stage, 0 : len(peers)]
        pltpu.make_async_copy(arrived, arrived, ar_rs.at[stage]).wait()
        return cur[stage, 0:1, :] + jnp.sum(slots[stage, 0 : len(peers), :], axis=0, keepdims=True)

    spread(0, jnp.where(lane_row == 3, packed + PENALTY * jnp.sum(mortar), packed), row)

    for i in range(CX):
        def second(c, _, i=i):
            mid, out, inner, here = stencil(W, i, c)
            V[i, here, :] = out
            return 0

        lax.fori_loop(0, CY // ROWS, second, 0)

    for q in (0, 1):
        add_left(q, left_jump(q, wait=False))
    add_right(jnp.concatenate([split(right_jump(q, wait=False)) for q in (2, 3)], axis=0), slice(2 * CY, 4 * CY))

    spread(1, collect(0, row), column)

    for q in (2, 3):
        add_left(q, left_jump(q))
        add_right(split(right_jump(q - 2)), slice((q - 2) * CY, (q - 1) * CY))

    total = collect(1, column)
    bb, bw, ww, wv = (total[0:1, n : n + 1] for n in range(4))
    alpha = bb / bw
    rr = alpha * alpha * ww - bb
    beta = rr / bb
    curve = bw - 2.0 * alpha * ww + alpha * alpha * wv - beta * beta * bw
    alpha2 = rr / curve
    scalars[0:8, :] = jnp.broadcast_to(alpha + alpha2 * (1.0 + beta), (8, 128))
    scalars[8:16, :] = jnp.broadcast_to(alpha * alpha2, (8, 128))

    for c in pairs_right + [b_up, b_down, ty_up] + w_inner + w_first + w_last + first_left + last_right + sl_right + psf_left:
        c.wait_send()
    for stage, peers in enumerate((row, column)):
        sent = slots.at[stage, 0 : len(peers)]
        pltpu.make_async_copy(sent, sent, ar_ss.at[stage]).wait()


def finish_kernel(B, W, V, scalars, x_hbm, r_hbm, x_v, r_v, sem):
    first, cross = scalars[0:1, 0:1], scalars[8:9, 0:1]
    out = []
    for i in range(CX):
        for h in range(2):
            n = 2 * i + h
            here, inner = pl.ds(h * ROWS, ROWS), pl.ds(PAD + h * ROWS, ROWS)
            b, w = B[i, inner, :], W[i, inner, :]
            x_v[i, here, :] = first * b - cross * w
            out.append(pltpu.make_async_copy(x_v.at[i, here], x_hbm.at[i, here], sem.at[0, n]))
            out[-1].start()
            r_v[i, here, :] = b - first * w + cross * V[i, here, :]
            out.append(pltpu.make_async_copy(r_v.at[i, here], r_hbm.at[i, here], sem.at[1, n]))
            out[-1].start()
    for c in out:
        c.wait()


def body(mesh, b, tx, ty, tz, st, perm, kind, count, proj):
    n_sub, n_blk = mesh.shape["sub"], mesh.shape["blk"]
    vm = lambda *shape, dtype=F32: pltpu.VMEM(shape, dtype)
    face, block, padded = (NFB, FB), (CX, CY, CZ), (CX, CY + 2 * PAD, CZ)
    scratch = [
        vm(*block), vm(CX, CY + PAD, CZ), vm(*block), vm(*block),
        vm(1, 1, NFB, dtype=I32), vm(1, 1, NFB, dtype=I32),
        vm(8, FB, dtype=I32),
        vm(1, 1, NFB, dtype=I32), vm(1, 1, NFB, dtype=I32), vm(8, FB, dtype=I32), vm(KINDS, FB, FB),
        vm(6 * FB, 2 * FB, dtype=BF16), vm(6 * FB, 2 * FB, dtype=BF16), vm(6 * FB, 2 * FB, dtype=BF16),
        vm(2, NFB, FB, dtype=I32), vm(2, NFB, FB, dtype=BF16), vm(*face),
        vm(NFB, NFB, dtype=BF16), vm(NFB, NFB, dtype=BF16), vm(NFB, NFB, dtype=BF16),
        vm(CY, CZ), vm(CY, CZ), vm(*face), vm(*face), vm(*face), vm(*face),
        vm(NFB, 2 * FB, dtype=BF16), vm(NFB, 2 * FB, dtype=BF16), vm(NFB, 2 * FB, dtype=BF16), vm(NFB, 2 * FB),
        vm(*face), vm(*face), vm(*face),
        vm(5, CX, 8, CZ), vm(2, 8, FB), vm(2, n_sub, FB), pltpu.SemaphoreType.REGULAR((7,)),
        pltpu.SemaphoreType.DMA((5, CX)), pltpu.SemaphoreType.DMA((3,)),
        pltpu.SemaphoreType.DMA((24,)), pltpu.SemaphoreType.DMA((24,)),
        pltpu.SemaphoreType.DMA((2,)), pltpu.SemaphoreType.DMA((2,)),
    ]
    like = lambda *shape: jax.ShapeDtypeStruct(shape, F32)
    in_vmem, in_hbm = pl.BlockSpec(memory_space=pltpu.VMEM), pl.BlockSpec(memory_space=pltpu.HBM)
    args = [pltpu.with_memory_space_constraint(a, pltpu.HBM) for a in (b, tx, ty, tz, st, perm, kind, proj)]
    state = pl.pallas_call(
        functools.partial(kernel, n_sub, n_blk),
        out_shape=(vm(*padded), vm(*padded), vm(*block), vm(16, 128)),
        in_specs=[in_hbm] * 8 + [pl.BlockSpec(memory_space=pltpu.SMEM)],
        out_specs=(in_vmem,) * 4,
        scratch_shapes=scratch,
        compiler_params=pltpu.CompilerParams(
            collective_id=0, has_side_effects=True, vmem_limit_bytes=48 * 1024 * 1024
        ),
        name="darcy_cg",
    )(*args, count)
    return tuple(pl.pallas_call(
        finish_kernel,
        out_shape=(like(*block), like(*block)),
        in_specs=[in_vmem] * 4,
        out_specs=(in_hbm,) * 2,
        scratch_shapes=[vm(*block), vm(*block), pltpu.SemaphoreType.DMA((2, 2 * CX))],
        compiler_params=pltpu.CompilerParams(vmem_limit_bytes=32 * 1024 * 1024),
        name="finish",
    )(*state))


def solution(mesh):
    cells = P("sub", "blk", None)
    return jax.shard_map(
        functools.partial(body, mesh), mesh=mesh,
        in_specs=(cells,) * 7 + (P("sub", "blk"), P()), out_specs=(cells, cells), check_vma=False,
    )
```

```python
import functools

import jax
import jax.numpy as jnp
from jax import lax
from jax.experimental import pallas as pl
from jax.experimental.pallas import tpu as pltpu
from jax.sharding import PartitionSpec as P

MESH = pl.DeviceIdType.MESH
F32, BF16, I32 = jnp.float32, jnp.bfloat16, jnp.int32
CX, CY, CZ = 4, 256, 512
FB, KINDS = 128, 4
GROUPS = CZ // FB
NFB = CY * GROUPS
PAD = 8
ROWS = 128
BAND = CY // GROUPS
PENALTY = 4.0


def split(x):
    high = x.astype(BF16)
    low = (x - high.astype(F32)).astype(BF16)
    return jnp.concatenate([high, low], axis=1)


def fold(x):
    total = None
    for r in range(0, x.shape[0], 8):
        for c in range(0, x.shape[1], 128):
            tile = x[r : r + 8, c : c + 128]
            total = tile if total is None else total + tile
    return total


def kernel(n_sub, n_blk, b_hbm, tx_hbm, ty_hbm, tz_hbm, st_hbm, perm_hbm, type_hbm, proj_hbm, count_s,
           B, W, V, scalars,
           TX, TY, TZ, ST,
           perm_v, type_v, count_v, perm_in, type_in, count_in, PROJ,
           wpt, wpp, wm, CB, LOW, NAT, GL, GR, GT,
           face_in, last_in, sl, sl_in, psf, psf_in,
           HL, HL2, HJ, ACC, C2L, J1R, C2R,
           edges, cur, slots, known,
           load_sem, small_sem, ss, rs, ar_ss, ar_rs):
    s, k = lax.axis_index("sub"), lax.axis_index("blk")
    right, left = (lax.rem(s + 1, n_sub), k), (lax.rem(s + n_sub - 1, n_sub), k)
    up, down = (s, lax.rem(k + 1, n_blk)), (s, lax.rem(k + n_blk - 1, n_blk))
    row = [(s, lax.rem(k + i, n_blk)) for i in range(1, n_blk)]
    line = 4
    x, z = lax.rem(s, line), s // line
    away = lambda d, size: min(d, size - d)
    plane = [(lax.rem(z + i, n_sub // line) * line + x, lax.rem(k + j, n_blk)) for i, j in sorted(
        ((i, j) for i in range(n_sub // line) for j in range(n_blk) if i or j),
        key=lambda o: (-away(o[0], n_sub // line) - away(o[1], n_blk) / 2, o))]
    in_line = [(z * line + lax.rem(x + i, line), k) for i in (2, 1, 3)]
    has_left, has_right, has_down, has_up = s > 0, s < n_sub - 1, k > 0, k < n_blk - 1

    def along(axis, distance):
        for step in (distance, -distance):
            here, size = (s, n_sub) if axis == "sub" else (k, n_blk)
            exists = here + step < size if step > 0 else here + step >= 0
            yield exists, ((s + step, k) if axis == "sub" else (s, k + step))

    def tell(axis, distance, semaphore):
        for exists, peer in along(axis, distance):
            @pl.when(exists)
            def _():
                pl.semaphore_signal(semaphore, inc=1, device_id=peer, device_id_type=MESH)

    def hear(axis, distance, semaphore):
        pl.semaphore_wait(semaphore, sum(exists.astype(I32) for exists, _ in along(axis, distance)))

    barrier = pltpu.get_barrier_semaphore()
    tell("sub", 1, barrier)
    tell("blk", 1, barrier)

    small = [
        pltpu.make_async_copy(perm_hbm, perm_v, small_sem.at[0]),
        pltpu.make_async_copy(type_hbm, type_v, small_sem.at[1]),
        pltpu.make_async_copy(proj_hbm, PROJ, small_sem.at[2]),
    ]
    for c in small:
        c.start()

    def load(a, i):
        src, dst = ((b_hbm, B), (tx_hbm, TX), (ty_hbm, TY), (tz_hbm, TZ), (st_hbm, ST))[a]
        to = dst.at[i, pl.ds(PAD, CY), :] if a in (0, 2) else dst.at[i]
        return pltpu.make_async_copy(src.at[i], to, load_sem.at[a, i])

    order = [(0, 3), (0, 2), (2, 3), (3, 3), (4, 3), (1, 2), (0, 0), (0, 1), (2, 0), (3, 0), (4, 0), (1, 0),
             (2, 1), (3, 1), (4, 1), (1, 1), (2, 2), (3, 2), (4, 2)]
    loads = {key: load(*key) for key in order}
    for key in order[:6]:
        loads[key].start()

    @pl.when(s == 0)
    def _():
        for ref in (perm_in, type_in, count_in):
            ref[...] = jnp.zeros_like(ref)
        last_in[...] = jnp.zeros_like(last_in)
        sl_in[...] = jnp.zeros_like(sl_in)

    @pl.when(s == n_sub - 1)
    def _():
        face_in[...] = jnp.zeros_like(face_in)
        psf_in[...] = jnp.zeros_like(psf_in)

    @pl.when(k == 0)
    def _():
        for n in (0, 2, 3):
            edges[n] = jnp.zeros((CX, 8, CZ), F32)

    @pl.when(k == n_blk - 1)
    def _():
        for n in (1, 4):
            edges[n] = jnp.zeros((CX, 8, CZ), F32)

    count_v[...] = jnp.full((8, FB), count_s[0, 0], I32)

    pl.semaphore_wait(barrier, sum(e.astype(I32) for e in (has_left, has_right, has_down, has_up)))

    class Send:
        def __init__(self, src, dst, n, to, sends, receives):
            self.sends, self.receives = sends, receives
            self.copy = pltpu.make_async_remote_copy(
                src_ref=src, dst_ref=dst, send_sem=ss.at[n], recv_sem=rs.at[n], device_id=to, device_id_type=MESH
            )

        def start(self):
            pl.when(self.sends)(self.copy.start)

        def wait_send(self):
            pl.when(self.sends)(self.copy.wait_send)

        def wait_recv(self):
            pl.when(self.receives)(self.copy.wait_recv)

    to_up, to_down = (up, has_up, has_down), (down, has_down, has_up)
    to_right, to_left = (right, has_right, has_left), (left, has_left, has_right)
    pairs_right = [Send(perm_hbm, perm_in, 0, *to_right), Send(type_hbm, type_in, 1, *to_right),
                   Send(count_v, count_in, 2, *to_right)]
    b_up = Send(b_hbm.at[:, CY - 1 : CY, :], edges.at[0, :, 0:1, :], 3, *to_up)
    b_down = Send(b_hbm.at[:, 0:1, :], edges.at[1, :, 0:1, :], 4, *to_down)
    ty_up = Send(ty_hbm.at[:, CY - 1 : CY, :], edges.at[2, :, 0:1, :], 5, *to_up)

    def w_edges(at, n):
        return [Send(W.at[at, PAD + CY - 1 : PAD + CY, :], edges.at[3, at, 0:1, :], n, *to_up),
                Send(W.at[at, PAD : PAD + 1, :], edges.at[4, at, 0:1, :], n + 1, *to_down)]

    w_inner, w_first, w_last = w_edges(pl.ds(1, 2), 6), w_edges(pl.ds(0, 1), 8), w_edges(pl.ds(3, 1), 10)
    quarter = [pl.ds(q * CY, CY) for q in range(GROUPS)]
    sl_right = [Send(sl.at[quarter[q]], sl_in.at[quarter[q]], 12 + q, *to_right) for q in range(GROUPS)]
    psf_left = [Send(psf.at[quarter[q]], psf_in.at[quarter[q]], 16 + q, *to_left) for q in range(GROUPS)]
    parts = [pl.ds(0, CY - BAND), pl.ds(CY - BAND, BAND)]
    first_left = [Send(b_hbm.at[0, p], face_in.at[p], 20 + n, *to_left) for n, p in enumerate(parts)]
    last_right = [Send(b_hbm.at[CX - 1, p], last_in.at[p], 22 + n, *to_right) for n, p in enumerate(parts)]

    for c in pairs_right:
        c.start()
    for n in range(2):
        first_left[n].start()
        last_right[n].start()
    b_up.start()
    b_down.start()
    ty_up.start()
    tell("sub", 1, known.at[0])
    tell("blk", 1, known.at[4])
    for key in order[6:]:
        loads[key].start()
    for c in small:
        c.wait()

    def place_matrix(target, t, matrix):
        high = matrix.astype(BF16)
        low = (matrix - high.astype(F32)).astype(BF16)
        at, base = slice((t % 2) * FB, (t % 2 + 1) * FB), t // 2
        target[base * 2 * FB : (base * 2 + 1) * FB, at] = high
        target[(base * 2 + 1) * FB : (base * 2 + 2) * FB, at] = high
        target[(4 + base) * FB : (5 + base) * FB, at] = low

    for t in range(KINDS):
        matrix = PROJ[t]
        turned = matrix.T
        place_matrix(wpt, t, turned)
        place_matrix(wpp, t, matrix)
        place_matrix(wm, t, jnp.dot(matrix, turned, precision=lax.Precision.HIGHEST, preferred_element_type=F32))

    lane = lax.broadcasted_iota(I32, (FB, FB), 1)
    sub_row = lax.broadcasted_iota(I32, (FB, FB), 0)

    def columns_of(perm_ref, type_ref, count_ref, side):
        for i in range(NFB // FB):
            at = slice(i * FB, (i + 1) * FB)
            perm = perm_ref[0, :, at]
            y = lax.shift_right_logical(perm, 2)
            place = (lax.shift_right_logical(y, 6) * CY + jnp.bitwise_and(perm, GROUPS - 1) * BAND
                     + jnp.bitwise_and(y, BAND - 1))
            live = (lax.broadcasted_iota(I32, (1, FB), 1) + i * FB < count_ref[0:1, :]).astype(I32)
            code = (place + type_ref[0, :, at] * NFB + live * (NFB * KINDS)).astype(F32)
            NAT[at, :] = jnp.broadcast_to(code, (FB, FB)).T
        for n in range(GROUPS * GROUPS):
            at = slice(n * BAND, (n + 1) * BAND)
            c = NAT[pl.ds((n // GROUPS) * CY + n % GROUPS, BAND, stride=GROUPS), :].astype(I32)
            CB[side, at, :] = c
            LOW[side, at, :] = jnp.where(jnp.bitwise_and(c, 2 * NFB) == 0, 1.0, 0.0).astype(BF16)

    def one_hot(side, G):
        def step(i, _):
            r = pl.multiple_of(i * FB, FB)
            place = jnp.bitwise_and(CB[side, pl.ds(r, FB), :], NFB - 1)
            for j in range(NFB // FB):
                G[pl.ds(r, FB), j * FB : (j + 1) * FB] = jnp.where(place == lane + j * FB, 1.0, 0.0).astype(BF16)
            return 0
        lax.fori_loop(0, NFB // FB, step, 0)

    def one_hot_back(side, G):
        for i in range(NFB // FB):
            place = jnp.bitwise_and(CB[side, i * FB : (i + 1) * FB, :], NFB - 1).astype(F32).T.astype(I32)
            def step(j, _):
                r = pl.multiple_of(j * FB, FB)
                G[pl.ds(r, FB), i * FB : (i + 1) * FB] = jnp.where(place == sub_row + r, 1.0, 0.0).astype(BF16)
                return 0
            lax.fori_loop(0, NFB // FB, step, 0)

    def live_of(side, at):
        return lax.shift_right_logical(CB[side, at, :], 12).astype(F32)

    def pieces(quarters):
        for c in quarters:
            for q in range(GROUPS):
                n = c * GROUPS + q
                yield (slice(n * BAND, (n + 1) * BAND), slice(c * BAND, (c + 1) * BAND), slice(q * FB, (q + 1) * FB),
                       slice(PAD + c * BAND, PAD + (c + 1) * BAND))

    def project(pair, target, side, at=slice(0, NFB)):
        low_kind = LOW[side, at, :]
        high_kind = 1.0 - low_kind
        high, low = pair[:, :FB], pair[:, FB:]
        ha, hb = high * low_kind, high * high_kind
        x = jnp.concatenate([ha, low * low_kind, hb, low * high_kind, ha, hb], axis=1)
        y = jnp.dot(x, target[...], preferred_element_type=F32)
        odd = jnp.bitwise_and(CB[side, at, :], NFB) != 0
        return jnp.where(odd, y[:, FB:], y[:, :FB])

    columns_of(perm_v, type_v, count_v, 0)
    one_hot(0, GL)

    def stencil(S, i, c):
        y = pl.multiple_of(c * ROWS, ROWS)
        here, inner = pl.ds(y, ROWS), pl.ds(pl.multiple_of(y + PAD, PAD), ROWS)
        big = S[i, pl.ds(y, ROWS + 2 * PAD), :]
        mid = big[PAD : PAD + ROWS]
        after = pltpu.roll(big, ROWS + 2 * PAD - 1, 0)
        flux = TY[i, pl.ds(y, ROWS + PAD), :] * (big[: PAD + ROWS] - after[: PAD + ROWS])
        out = ST[i, here, :] * mid + (flux[PAD:] - pltpu.roll(flux, 1, 0)[PAD:])
        flux = TZ[i, here, :] * (mid - pltpu.roll(mid, CZ - 1, 1))
        out = out + (flux - pltpu.roll(flux, 1, 1))
        if i < CX - 1:
            out = out + TX[i, here, :] * (mid - S[i + 1, inner, :])
        if i > 0:
            out = out - TX[i - 1, here, :] * (S[i - 1, inner, :] - mid)
        return mid, out, inner, here

    def energy(i, along_x):
        W[i, PAD + CY : PAD + CY + 1, :] = W[i, PAD + CY - 1 : PAD + CY, :]

        def step(c, acc):
            y = pl.multiple_of(c * ROWS, ROWS)
            here, inner = pl.ds(y, ROWS), pl.ds(pl.multiple_of(y + PAD, PAD), ROWS)
            big = W[i, pl.ds(pl.multiple_of(y + PAD, PAD), ROWS + PAD), :]
            mid = big[:ROWS]
            d = mid - pltpu.roll(big, ROWS + PAD - 1, 0)[:ROWS]
            e = ST[i, here, :] * mid * mid + TY[i, inner, :] * d * d
            d = mid - pltpu.roll(mid, CZ - 1, 1)
            e = e + TZ[i, here, :] * d * d
            if along_x:
                d = mid - W[i + 1, inner, :]
                e = e + TX[i, here, :] * d * d
            if i == CX - 1:
                d = W[i - 1, inner, :] - mid
                e = e + TX[i - 1, here, :] * d * d
            return acc + fold(e)

        return lambda acc: lax.fori_loop(0, CY // ROWS, step, acc)

    def prepare(i):
        edge = TZ[i, :, CZ - FB :]
        TZ[i, :, CZ - FB :] = jnp.where(lax.broadcasted_iota(I32, (CY, FB), 1) == FB - 1, 0.0, edge)
        TY[i, PAD + CY - 1 : PAD + CY, :] = jnp.where(has_up, TY[i, PAD + CY - 1 : PAD + CY, :], 0.0)
        TY[i, PAD - 1 : PAD, :] = edges[2, i, 0:1, :]
        B[i, PAD - 1 : PAD, :] = edges[0, i, 0:1, :]
        B[i, PAD + CY : PAD + CY + 1, :] = edges[1, i, 0:1, :]

    for a, i in order[:6]:
        loads[a, i].wait()
    b_up.wait_recv()
    b_down.wait_recv()
    ty_up.wait_recv()
    prepare(3)

    def last_face(c, _):
        mid, out, inner, here = stencil(B, 3, c)
        W[3, inner, :] = out
        for n in range(ROWS // BAND * GROUPS):
            h, q = divmod(n, GROUPS)
            at = pl.ds(pl.multiple_of(c * (ROWS * GROUPS) + n * BAND, BAND), BAND)
            sl[at, :] = out[h * BAND : (h + 1) * BAND, q * FB : (q + 1) * FB]
        return 0

    lax.fori_loop(0, CY // ROWS, last_face, 0)
    for q in (2, 3):
        sl_right[q].start()

    hear("sub", 1, known.at[0])
    tell("sub", 2, known.at[1])
    hear("blk", 1, known.at[4])
    tell("blk", 2, known.at[5])

    for a, i in order[6:12]:
        loads[a, i].wait()
    prepare(0)

    def first_face(c, _):
        mid, out, inner, here = stencil(B, 0, c)
        W[0, inner, :] = out
        for n in range(ROWS // BAND * GROUPS):
            h, q = divmod(n, GROUPS)
            at = pl.ds(pl.multiple_of(c * (ROWS * GROUPS) + n * BAND, BAND), BAND)
            ys, cols = slice(h * BAND, (h + 1) * BAND), slice(q * FB, (q + 1) * FB)
            HL[at, :] = split(mid[ys, cols])
            HL2[at, :] = split(out[ys, cols])
        return 0

    lax.fori_loop(0, CY // ROWS, first_face, 0)

    for c in pairs_right:
        c.wait_recv()
    columns_of(perm_in, type_in, count_in, 1)
    one_hot(1, GR)
    g = jnp.dot(GR[...], HL2[...], preferred_element_type=F32).astype(BF16)
    psf[...] = project(g, wpt, 1)
    for q in (0, 1):
        psf_left[q].start()
    hear("sub", 2, known.at[1])
    tell("sub", 4, known.at[2])
    hear("blk", 2, known.at[5])
    tell("blk", 4, known.at[6])
    g = jnp.dot(GR[...], HL[...], preferred_element_type=F32).astype(BF16)
    J1R[...] = project(g, wpt, 1)

    hear("sub", 4, known.at[2])
    tell("sub", 8, known.at[3])
    one_hot_back(1, GT)

    for a, i in order[12:]:
        loads[a, i].wait()
    zero = jnp.zeros((8, 128), F32)
    sums = (zero, zero, zero)
    for i in (1, 2):
        prepare(i)

        def middle(c, acc, i=i):
            mid, out, inner, here = stencil(B, i, c)
            W[i, inner, :] = out
            return acc[0] + fold(mid * mid), acc[1] + fold(mid * out), acc[2] + fold(out * out)

        sums = lax.fori_loop(0, CY // ROWS, middle, sums)
    for c in w_inner:
        c.start()
    hear("sub", 8, known.at[3])
    hear("blk", 4, known.at[6])
    for peer in row:
        pl.semaphore_signal(known.at[7], inc=1, device_id=peer, device_id_type=MESH)
    wv = energy(1, True)(zero)
    wv = energy(2, False)(wv)

    right_one, left_one = has_right.astype(F32), has_left.astype(F32)
    most, rest = slice(0, NFB - CY), slice(NFB - CY, NFB)

    def gather_right(quarters, at):
        for rows, ys, cols, _ in pieces(quarters):
            HL[rows, :] = split(face_in[ys, cols])
        return jnp.dot(GL[:, at], HL[at, :], preferred_element_type=F32)

    def jumps_left(quarters, at):
        for rows, ys, cols, _ in pieces(quarters):
            jump = left_one * live_of(1, rows) * (last_in[ys, cols] - J1R[rows, :])
            HJ[rows, :] = split(jump)
            C2R[rows, :] = PENALTY * jump - psf[rows, :]
        HL2[at, :] = split(project(HJ[at, :], wpp, 1, at))
        return jnp.dot(GT[:, at], HL2[at, :], preferred_element_type=F32)

    first_left[0].wait_recv()
    last_right[0].wait_recv()
    ACC[...] = gather_right((0, 1, 2), most)
    g = jumps_left((0, 1, 2), most)
    for at, _, cols, ys in pieces(range(GROUPS)):
        W[0, ys, cols] = W[0, ys, cols] - PENALTY * (g[at, :FB] + g[at, FB:])
    first_left[1].wait_recv()
    last_right[1].wait_recv()
    g = jumps_left((3,), rest)
    for at, _, cols, ys in pieces(range(GROUPS)):
        w = W[0, ys, cols] - PENALTY * (g[at, :FB] + g[at, FB:])
        W[0, ys, cols] = w
        mid = B[0, ys, cols]
        sums = sums[0] + fold(mid * mid), sums[1] + fold(mid * w), sums[2] + fold(w * w)
    for c in w_first:
        c.start()
    g = ACC[...] + gather_right((3,), rest)
    projected = project(g.astype(BF16), wpt, 0)
    for at, _, cols, ys in pieces(range(GROUPS)):
        mid = B[3, ys, cols]
        jump = live_of(0, at) * (mid - projected[at])
        w = W[3, ys, cols] + PENALTY * jump
        W[3, ys, cols] = w
        HL[at, :] = split(jump)
        C2L[at, :] = w
        sums = sums[0] + fold(mid * mid), sums[1] + fold(mid * w), sums[2] + fold(w * w)

    for c in w_last:
        c.start()

    C2L[...] = C2L[...] + (PENALTY * right_one) * project(HL[...], wm, 0)
    C2R[...] = C2R[...] + PENALTY * project(HJ[...], wm, 1)
    wv = energy(0, True)(wv)
    wv = energy(3, False)(wv)

    def left_jump(q, wait=True):
        at = slice(q * CY, (q + 1) * CY)
        if wait:
            psf_left[q].wait_recv()
        return live_of(0, at) * (C2L[at, :] - psf_in[at, :])

    def right_jump(q, wait=True):
        at = slice(q * CY, (q + 1) * CY)
        if wait:
            sl_right[q].wait_recv()
        return left_one * live_of(1, at) * (sl_in[at, :] + C2R[at, :])

    def add_left(q, jump):
        for at, ys, cols, _ in pieces((q,)):
            V[3, ys, cols] = V[3, ys, cols] + PENALTY * jump[at.start - q * CY : at.stop - q * CY]

    def add_right(pair, at):
        back = split(project(pair, wpp, 1, at))
        g = jnp.dot(GT[:, at], back, preferred_element_type=F32)
        for rows, ys, cols, _ in pieces(range(GROUPS)):
            V[0, ys, cols] = V[0, ys, cols] - PENALTY * (g[rows, :FB] + g[rows, FB:])

    mortar = zero
    for q in (2, 3):
        at = slice(q * CY, (q + 1) * CY)
        only = live_of(0, at) * C2L[at, :]
        mortar = mortar + (1.0 - right_one) * fold(only * only)
    pl.semaphore_wait(known.at[7], n_blk - 1)
    for c in w_inner + w_first + w_last:
        c.wait_recv()
    across = jnp.zeros((1, CZ), F32)
    for i in range(CX):
        d = W[i, PAD + CY - 1 : PAD + CY, :] - edges[4, i, 0:1, :]
        across = across + TY[i, PAD + CY - 1 : PAD + CY, :] * d * d
        W[i, PAD - 1 : PAD, :] = edges[3, i, 0:1, :]
        W[i, PAD + CY : PAD + CY + 1, :] = edges[4, i, 0:1, :]
    lane_row = lax.broadcasted_iota(I32, (1, FB), 1)
    packed = jnp.zeros((1, FB), F32)
    for n, part in enumerate(sums):
        packed = jnp.where(lane_row == n, jnp.sum(part), packed)
    packed = jnp.where(lane_row == 3, jnp.sum(wv) + jnp.sum(across), packed)
    for n in range(2):
        jump = left_jump(n)
        mortar = mortar + fold(jump * jump)
        jump = right_jump(2 + n)
        mortar = mortar + fold(jump * jump)

    def spread(stage, part, peers):
        cur[stage, 0:1, :] = part
        for n, peer in enumerate(peers):
            pltpu.make_async_remote_copy(
                src_ref=cur.at[stage, 0:1], dst_ref=slots.at[stage, n : n + 1],
                send_sem=ar_ss.at[stage], recv_sem=ar_rs.at[stage], device_id=peer, device_id_type=MESH,
            ).start()

    def collect(stage, peers):
        arrived = slots.at[stage, 0 : len(peers)]
        pltpu.make_async_copy(arrived, arrived, ar_rs.at[stage]).wait()
        return cur[stage, 0:1, :] + jnp.sum(slots[stage, 0 : len(peers), :], axis=0, keepdims=True)

    spread(0, jnp.where(lane_row == 3, packed + PENALTY * jnp.sum(mortar), packed), plane)

    for q in (0, 1):
        sl_right[q].start()
        psf_left[q + 2].start()

    for i in range(CX):
        def second(c, _, i=i):
            mid, out, inner, here = stencil(W, i, c)
            V[i, here, :] = out
            return 0

        lax.fori_loop(0, CY // ROWS, second, 0)

    for q in (0, 1):
        add_left(q, left_jump(q, wait=False))
    add_right(jnp.concatenate([split(right_jump(q, wait=False)) for q in (2, 3)], axis=0), slice(2 * CY, 4 * CY))

    spread(1, collect(0, plane), in_line)

    for q in (2, 3):
        add_left(q, left_jump(q))
        add_right(split(right_jump(q - 2)), slice((q - 2) * CY, (q - 1) * CY))

    total = collect(1, in_line)
    bb, bw, ww, wv = (total[0:1, n : n + 1] for n in range(4))
    alpha = bb / bw
    rr = alpha * alpha * ww - bb
    beta = rr / bb
    curve = bw - 2.0 * alpha * ww + alpha * alpha * wv - beta * beta * bw
    alpha2 = rr / curve
    scalars[0:8, :] = jnp.broadcast_to(alpha + alpha2 * (1.0 + beta), (8, 128))
    scalars[8:16, :] = jnp.broadcast_to(alpha * alpha2, (8, 128))

    for c in pairs_right + [b_up, b_down, ty_up] + w_inner + w_first + w_last + first_left + last_right + sl_right + psf_left:
        c.wait_send()
    for stage, peers in enumerate((plane, in_line)):
        sent = slots.at[stage, 0 : len(peers)]
        pltpu.make_async_copy(sent, sent, ar_ss.at[stage]).wait()


def finish_kernel(B, W, V, scalars, x_hbm, r_hbm, x_v, r_v, sem):
    first, cross = scalars[0:1, 0:1], scalars[8:9, 0:1]
    out = []
    for i in range(CX):
        for h in range(2):
            n = 2 * i + h
            here, inner = pl.ds(h * ROWS, ROWS), pl.ds(PAD + h * ROWS, ROWS)
            b, w = B[i, inner, :], W[i, inner, :]
            x_v[i, here, :] = first * b - cross * w
            out.append(pltpu.make_async_copy(x_v.at[i, here], x_hbm.at[i, here], sem.at[0, n]))
            out[-1].start()
            r_v[i, here, :] = b - first * w + cross * V[i, here, :]
            out.append(pltpu.make_async_copy(r_v.at[i, here], r_hbm.at[i, here], sem.at[1, n]))
            out[-1].start()
    for c in out:
        c.wait()


def body(mesh, b, tx, ty, tz, st, perm, kind, count, proj):
    n_sub, n_blk = mesh.shape["sub"], mesh.shape["blk"]
    vm = lambda *shape, dtype=F32: pltpu.VMEM(shape, dtype)
    face, block, padded = (NFB, FB), (CX, CY, CZ), (CX, CY + 2 * PAD, CZ)
    scratch = [
        vm(*block), vm(CX, CY + PAD, CZ), vm(*block), vm(*block),
        vm(1, 1, NFB, dtype=I32), vm(1, 1, NFB, dtype=I32),
        vm(8, FB, dtype=I32),
        vm(1, 1, NFB, dtype=I32), vm(1, 1, NFB, dtype=I32), vm(8, FB, dtype=I32), vm(KINDS, FB, FB),
        vm(6 * FB, 2 * FB, dtype=BF16), vm(6 * FB, 2 * FB, dtype=BF16), vm(6 * FB, 2 * FB, dtype=BF16),
        vm(2, NFB, FB, dtype=I32), vm(2, NFB, FB, dtype=BF16), vm(*face),
        vm(NFB, NFB, dtype=BF16), vm(NFB, NFB, dtype=BF16), vm(NFB, NFB, dtype=BF16),
        vm(CY, CZ), vm(CY, CZ), vm(*face), vm(*face), vm(*face), vm(*face),
        vm(NFB, 2 * FB, dtype=BF16), vm(NFB, 2 * FB, dtype=BF16), vm(NFB, 2 * FB, dtype=BF16), vm(NFB, 2 * FB),
        vm(*face), vm(*face), vm(*face),
        vm(5, CX, 8, CZ), vm(2, 8, FB), vm(2, 32, FB), pltpu.SemaphoreType.REGULAR((8,)),
        pltpu.SemaphoreType.DMA((5, CX)), pltpu.SemaphoreType.DMA((3,)),
        pltpu.SemaphoreType.DMA((24,)), pltpu.SemaphoreType.DMA((24,)),
        pltpu.SemaphoreType.DMA((2,)), pltpu.SemaphoreType.DMA((2,)),
    ]
    like = lambda *shape: jax.ShapeDtypeStruct(shape, F32)
    in_vmem, in_hbm = pl.BlockSpec(memory_space=pltpu.VMEM), pl.BlockSpec(memory_space=pltpu.HBM)
    args = [pltpu.with_memory_space_constraint(a, pltpu.HBM) for a in (b, tx, ty, tz, st, perm, kind, proj)]
    state = pl.pallas_call(
        functools.partial(kernel, n_sub, n_blk),
        out_shape=(vm(*padded), vm(*padded), vm(*block), vm(16, 128)),
        in_specs=[in_hbm] * 8 + [pl.BlockSpec(memory_space=pltpu.SMEM)],
        out_specs=(in_vmem,) * 4,
        scratch_shapes=scratch,
        compiler_params=pltpu.CompilerParams(
            collective_id=0, has_side_effects=True, vmem_limit_bytes=48 * 1024 * 1024
        ),
        name="darcy_cg",
    )(*args, count)
    return tuple(pl.pallas_call(
        finish_kernel,
        out_shape=(like(*block), like(*block)),
        in_specs=[in_vmem] * 4,
        out_specs=(in_hbm,) * 2,
        scratch_shapes=[vm(*block), vm(*block), pltpu.SemaphoreType.DMA((2, 2 * CX))],
        compiler_params=pltpu.CompilerParams(vmem_limit_bytes=32 * 1024 * 1024),
        name="finish",
    )(*state))


def solution(mesh):
    cells = P("sub", "blk", None)
    return jax.shard_map(
        functools.partial(body, mesh), mesh=mesh,
        in_specs=(cells,) * 7 + (P("sub", "blk"), P()), out_specs=(cells, cells), check_vma=False,
    )
```

```python
import functools

import jax
import jax.numpy as jnp
from jax import lax
from jax.experimental import pallas as pl
from jax.experimental.pallas import tpu as pltpu
from jax.sharding import PartitionSpec as P

MESH = pl.DeviceIdType.MESH
F32, BF16, I32 = jnp.float32, jnp.bfloat16, jnp.int32
CX, CY, CZ = 4, 256, 512
FB, KINDS = 128, 4
GROUPS = CZ // FB
NFB = CY * GROUPS
PAD = 8
ROWS = 128
BAND = CY // GROUPS
PENALTY = 4.0


def split(x):
    high = x.astype(BF16)
    low = (x - high.astype(F32)).astype(BF16)
    return jnp.concatenate([high, low], axis=1)


def fold(x):
    total = None
    for r in range(0, x.shape[0], 8):
        for c in range(0, x.shape[1], 128):
            tile = x[r : r + 8, c : c + 128]
            total = tile if total is None else total + tile
    return total


def kernel(n_sub, n_blk, b_hbm, tx_hbm, ty_hbm, tz_hbm, st_hbm, perm_hbm, type_hbm, proj_hbm, count_s,
           B, W, V, scalars,
           TX, TY, TZ, ST,
           perm_v, type_v, count_v, perm_in, type_in, count_in, PROJ,
           wpt, wpp, wm, CB, LOW, NAT, GL, GR, GT,
           face_in, last_in, sl, sl_in, psf, psf_in,
           HL, HL2, HJ, ACC, C2L, J1R, C2R,
           edges, cur, slots, known,
           load_sem, small_sem, ss, rs, ar_ss, ar_rs):
    s, k = lax.axis_index("sub"), lax.axis_index("blk")
    right, left = (lax.rem(s + 1, n_sub), k), (lax.rem(s + n_sub - 1, n_sub), k)
    up, down = (s, lax.rem(k + 1, n_blk)), (s, lax.rem(k + n_blk - 1, n_blk))
    row = [(s, lax.rem(k + i, n_blk)) for i in range(1, n_blk)]
    line = 4
    x, z = lax.rem(s, line), s // line
    away = lambda d, size: min(d, size - d)
    plane = [(lax.rem(z + i, n_sub // line) * line + x, lax.rem(k + j, n_blk)) for i, j in sorted(
        ((i, j) for i in range(n_sub // line) for j in range(n_blk) if i or j),
        key=lambda o: (-away(o[0], n_sub // line) - away(o[1], n_blk) / 2, o))]
    in_line = [(z * line + lax.rem(x + i, line), k) for i in (2, 1, 3)]
    has_left, has_right, has_down, has_up = s > 0, s < n_sub - 1, k > 0, k < n_blk - 1

    def along(axis, distance):
        for step in (distance, -distance):
            here, size = (s, n_sub) if axis == "sub" else (k, n_blk)
            exists = here + step < size if step > 0 else here + step >= 0
            yield exists, ((s + step, k) if axis == "sub" else (s, k + step))

    def tell(axis, distance, semaphore):
        for exists, peer in along(axis, distance):
            @pl.when(exists)
            def _():
                pl.semaphore_signal(semaphore, inc=1, device_id=peer, device_id_type=MESH)

    def hear(axis, distance, semaphore):
        pl.semaphore_wait(semaphore, sum(exists.astype(I32) for exists, _ in along(axis, distance)))

    barrier = pltpu.get_barrier_semaphore()
    tell("sub", 1, barrier)
    tell("blk", 1, barrier)

    small = [
        pltpu.make_async_copy(perm_hbm, perm_v, small_sem.at[0]),
        pltpu.make_async_copy(type_hbm, type_v, small_sem.at[1]),
        pltpu.make_async_copy(proj_hbm, PROJ, small_sem.at[2]),
    ]
    for c in small:
        c.start()

    def load(a, i):
        src, dst = ((b_hbm, B), (tx_hbm, TX), (ty_hbm, TY), (tz_hbm, TZ), (st_hbm, ST))[a]
        to = dst.at[i, pl.ds(PAD, CY), :] if a in (0, 2) else dst.at[i]
        return pltpu.make_async_copy(src.at[i], to, load_sem.at[a, i])

    order = [(0, 3), (0, 2), (2, 3), (3, 3), (4, 3), (1, 2), (0, 0), (0, 1), (2, 0), (3, 0), (4, 0), (1, 0),
             (2, 1), (3, 1), (4, 1), (1, 1), (2, 2), (3, 2), (4, 2)]
    loads = {key: load(*key) for key in order}
    for key in order[:6]:
        loads[key].start()

    count_v[...] = jnp.full((8, FB), count_s[0, 0], I32)

    pl.semaphore_wait(barrier, sum(e.astype(I32) for e in (has_left, has_right, has_down, has_up)))

    class Send:
        def __init__(self, src, dst, n, to, sends, receives):
            self.sends, self.receives = sends, receives
            self.copy = pltpu.make_async_remote_copy(
                src_ref=src, dst_ref=dst, send_sem=ss.at[n], recv_sem=rs.at[n], device_id=to, device_id_type=MESH
            )

        def start(self):
            pl.when(self.sends)(self.copy.start)

        def wait_send(self):
            pl.when(self.sends)(self.copy.wait_send)

        def wait_recv(self):
            pl.when(self.receives)(self.copy.wait_recv)

    to_up, to_down = (up, has_up, has_down), (down, has_down, has_up)
    to_right, to_left = (right, has_right, has_left), (left, has_left, has_right)
    pairs_right = [Send(perm_hbm, perm_in, 0, *to_right), Send(type_hbm, type_in, 1, *to_right),
                   Send(count_v, count_in, 2, *to_right)]
    b_up = Send(b_hbm.at[:, CY - 1 : CY, :], edges.at[0, :, 0:1, :], 3, *to_up)
    b_down = Send(b_hbm.at[:, 0:1, :], edges.at[1, :, 0:1, :], 4, *to_down)
    ty_up = Send(ty_hbm.at[:, CY - 1 : CY, :], edges.at[2, :, 0:1, :], 5, *to_up)

    def w_edges(at, n):
        return [Send(W.at[at, PAD + CY - 1 : PAD + CY, :], edges.at[3, at, 0:1, :], n, *to_up),
                Send(W.at[at, PAD : PAD + 1, :], edges.at[4, at, 0:1, :], n + 1, *to_down)]

    w_inner, w_first, w_last = w_edges(pl.ds(1, 2), 6), w_edges(pl.ds(0, 1), 8), w_edges(pl.ds(3, 1), 10)
    quarter = [pl.ds(q * CY, CY) for q in range(GROUPS)]
    sl_right = [Send(sl.at[quarter[q]], sl_in.at[quarter[q]], 12 + q, *to_right) for q in range(GROUPS)]
    psf_left = [Send(psf.at[quarter[q]], psf_in.at[quarter[q]], 16 + q, *to_left) for q in range(GROUPS)]
    parts = [pl.ds(0, CY - BAND), pl.ds(CY - BAND, BAND)]
    first_left = [Send(b_hbm.at[0, p], face_in.at[p], 20 + n, *to_left) for n, p in enumerate(parts)]
    last_right = [Send(b_hbm.at[CX - 1, p], last_in.at[p], 22 + n, *to_right) for n, p in enumerate(parts)]

    for c in pairs_right:
        c.start()
    for n in range(2):
        first_left[n].start()
        last_right[n].start()
    b_up.start()
    b_down.start()
    ty_up.start()
    tell("sub", 1, known.at[0])
    tell("blk", 1, known.at[4])
    for key in order[6:]:
        loads[key].start()
    for c in small:
        c.wait()

    @pl.when(s == 0)
    def _():
        for ref in (perm_in, type_in, count_in):
            ref[...] = jnp.zeros_like(ref)
        last_in[...] = jnp.zeros_like(last_in)
        sl_in[...] = jnp.zeros_like(sl_in)

    @pl.when(s == n_sub - 1)
    def _():
        face_in[...] = jnp.zeros_like(face_in)
        psf_in[...] = jnp.zeros_like(psf_in)

    @pl.when(k == 0)
    def _():
        for n in (0, 2, 3):
            edges[n] = jnp.zeros((CX, 8, CZ), F32)

    @pl.when(k == n_blk - 1)
    def _():
        for n in (1, 4):
            edges[n] = jnp.zeros((CX, 8, CZ), F32)

    def place_matrix(target, t, matrix):
        high = matrix.astype(BF16)
        low = (matrix - high.astype(F32)).astype(BF16)
        at, base = slice((t % 2) * FB, (t % 2 + 1) * FB), t // 2
        target[base * 2 * FB : (base * 2 + 1) * FB, at] = high
        target[(base * 2 + 1) * FB : (base * 2 + 2) * FB, at] = high
        target[(4 + base) * FB : (5 + base) * FB, at] = low

    for t in range(KINDS):
        matrix = PROJ[t]
        turned = matrix.T
        place_matrix(wpt, t, turned)
        place_matrix(wpp, t, matrix)
        place_matrix(wm, t, jnp.dot(matrix, turned, precision=lax.Precision.HIGHEST, preferred_element_type=F32))

    lane = lax.broadcasted_iota(I32, (FB, FB), 1)
    sub_row = lax.broadcasted_iota(I32, (FB, FB), 0)

    def columns_of(perm_ref, type_ref, count_ref, side):
        for i in range(NFB // FB):
            at = slice(i * FB, (i + 1) * FB)
            perm = perm_ref[0, :, at]
            y = lax.shift_right_logical(perm, 2)
            place = (lax.shift_right_logical(y, 6) * CY + jnp.bitwise_and(perm, GROUPS - 1) * BAND
                     + jnp.bitwise_and(y, BAND - 1))
            live = (lax.broadcasted_iota(I32, (1, FB), 1) + i * FB < count_ref[0:1, :]).astype(I32)
            code = (place + type_ref[0, :, at] * NFB + live * (NFB * KINDS)).astype(F32)
            NAT[at, :] = jnp.broadcast_to(code, (FB, FB)).T
        for n in range(GROUPS * GROUPS):
            at = slice(n * BAND, (n + 1) * BAND)
            c = NAT[pl.ds((n // GROUPS) * CY + n % GROUPS, BAND, stride=GROUPS), :].astype(I32)
            CB[side, at, :] = c
            LOW[side, at, :] = jnp.where(jnp.bitwise_and(c, 2 * NFB) == 0, 1.0, 0.0).astype(BF16)

    def one_hot(side, G):
        def step(i, _):
            r = pl.multiple_of(i * FB, FB)
            place = jnp.bitwise_and(CB[side, pl.ds(r, FB), :], NFB - 1)
            for j in range(NFB // FB):
                G[pl.ds(r, FB), j * FB : (j + 1) * FB] = jnp.where(place == lane + j * FB, 1.0, 0.0).astype(BF16)
            return 0
        lax.fori_loop(0, NFB // FB, step, 0)

    def one_hot_back(side, G):
        for i in range(NFB // FB):
            place = jnp.bitwise_and(CB[side, i * FB : (i + 1) * FB, :], NFB - 1).astype(F32).T.astype(I32)
            def step(j, _):
                r = pl.multiple_of(j * FB, FB)
                G[pl.ds(r, FB), i * FB : (i + 1) * FB] = jnp.where(place == sub_row + r, 1.0, 0.0).astype(BF16)
                return 0
            lax.fori_loop(0, NFB // FB, step, 0)

    def live_of(side, at):
        return lax.shift_right_logical(CB[side, at, :], 12).astype(F32)

    def pieces(quarters):
        for c in quarters:
            for q in range(GROUPS):
                n = c * GROUPS + q
                yield (slice(n * BAND, (n + 1) * BAND), slice(c * BAND, (c + 1) * BAND), slice(q * FB, (q + 1) * FB),
                       slice(PAD + c * BAND, PAD + (c + 1) * BAND))

    def project(pair, target, side, at=slice(0, NFB)):
        low_kind = LOW[side, at, :]
        high_kind = 1.0 - low_kind
        high, low = pair[:, :FB], pair[:, FB:]
        ha, hb = high * low_kind, high * high_kind
        x = jnp.concatenate([ha, low * low_kind, hb, low * high_kind, ha, hb], axis=1)
        y = jnp.dot(x, target[...], preferred_element_type=F32)
        odd = jnp.bitwise_and(CB[side, at, :], NFB) != 0
        return jnp.where(odd, y[:, FB:], y[:, :FB])

    columns_of(perm_v, type_v, count_v, 0)
    one_hot(0, GL)

    def stencil(S, i, c):
        y = pl.multiple_of(c * ROWS, ROWS)
        here, inner = pl.ds(y, ROWS), pl.ds(pl.multiple_of(y + PAD, PAD), ROWS)
        big = S[i, pl.ds(y, ROWS + 2 * PAD), :]
        mid = big[PAD : PAD + ROWS]
        after = pltpu.roll(big, ROWS + 2 * PAD - 1, 0)
        flux = TY[i, pl.ds(y, ROWS + PAD), :] * (big[: PAD + ROWS] - after[: PAD + ROWS])
        out = ST[i, here, :] * mid + (flux[PAD:] - pltpu.roll(flux, 1, 0)[PAD:])
        flux = TZ[i, here, :] * (mid - pltpu.roll(mid, CZ - 1, 1))
        out = out + (flux - pltpu.roll(flux, 1, 1))
        if i < CX - 1:
            out = out + TX[i, here, :] * (mid - S[i + 1, inner, :])
        if i > 0:
            out = out - TX[i - 1, here, :] * (S[i - 1, inner, :] - mid)
        return mid, out, inner, here

    def energy(i, along_x):
        W[i, PAD + CY : PAD + CY + 1, :] = W[i, PAD + CY - 1 : PAD + CY, :]

        def step(c, acc):
            y = pl.multiple_of(c * ROWS, ROWS)
            here, inner = pl.ds(y, ROWS), pl.ds(pl.multiple_of(y + PAD, PAD), ROWS)
            big = W[i, pl.ds(pl.multiple_of(y + PAD, PAD), ROWS + PAD), :]
            mid = big[:ROWS]
            d = mid - pltpu.roll(big, ROWS + PAD - 1, 0)[:ROWS]
            e = ST[i, here, :] * mid * mid + TY[i, inner, :] * d * d
            d = mid - pltpu.roll(mid, CZ - 1, 1)
            e = e + TZ[i, here, :] * d * d
            if along_x:
                d = mid - W[i + 1, inner, :]
                e = e + TX[i, here, :] * d * d
            if i == CX - 1:
                d = W[i - 1, inner, :] - mid
                e = e + TX[i - 1, here, :] * d * d
            return acc + fold(e)

        return lambda acc: lax.fori_loop(0, CY // ROWS, step, acc)

    def prepare(i):
        edge = TZ[i, :, CZ - FB :]
        TZ[i, :, CZ - FB :] = jnp.where(lax.broadcasted_iota(I32, (CY, FB), 1) == FB - 1, 0.0, edge)
        TY[i, PAD + CY - 1 : PAD + CY, :] = jnp.where(has_up, TY[i, PAD + CY - 1 : PAD + CY, :], 0.0)
        TY[i, PAD - 1 : PAD, :] = edges[2, i, 0:1, :]
        B[i, PAD - 1 : PAD, :] = edges[0, i, 0:1, :]
        B[i, PAD + CY : PAD + CY + 1, :] = edges[1, i, 0:1, :]

    for a, i in order[:6]:
        loads[a, i].wait()
    b_up.wait_recv()
    b_down.wait_recv()
    ty_up.wait_recv()
    prepare(3)

    def last_face(c, _):
        mid, out, inner, here = stencil(B, 3, c)
        W[3, inner, :] = out
        for n in range(ROWS // BAND * GROUPS):
            h, q = divmod(n, GROUPS)
            at = pl.ds(pl.multiple_of(c * (ROWS * GROUPS) + n * BAND, BAND), BAND)
            sl[at, :] = out[h * BAND : (h + 1) * BAND, q * FB : (q + 1) * FB]
        return 0

    lax.fori_loop(0, CY // ROWS, last_face, 0)
    for q in (2, 3):
        sl_right[q].start()

    hear("sub", 1, known.at[0])
    tell("sub", 2, known.at[1])
    hear("blk", 1, known.at[4])
    tell("blk", 2, known.at[5])

    for a, i in order[6:12]:
        loads[a, i].wait()
    prepare(0)

    def first_face(c, _):
        mid, out, inner, here = stencil(B, 0, c)
        W[0, inner, :] = out
        for n in range(ROWS // BAND * GROUPS):
            h, q = divmod(n, GROUPS)
            at = pl.ds(pl.multiple_of(c * (ROWS * GROUPS) + n * BAND, BAND), BAND)
            ys, cols = slice(h * BAND, (h + 1) * BAND), slice(q * FB, (q + 1) * FB)
            HL[at, :] = split(mid[ys, cols])
            HL2[at, :] = split(out[ys, cols])
        return 0

    lax.fori_loop(0, CY // ROWS, first_face, 0)

    for c in pairs_right:
        c.wait_recv()
    columns_of(perm_in, type_in, count_in, 1)
    one_hot(1, GR)
    g = jnp.dot(GR[...], HL2[...], preferred_element_type=F32).astype(BF16)
    psf[...] = project(g, wpt, 1)
    for q in (0, 1):
        psf_left[q].start()
    hear("sub", 2, known.at[1])
    tell("sub", 4, known.at[2])
    hear("blk", 2, known.at[5])
    tell("blk", 4, known.at[6])
    g = jnp.dot(GR[...], HL[...], preferred_element_type=F32).astype(BF16)
    J1R[...] = project(g, wpt, 1)

    hear("sub", 4, known.at[2])
    tell("sub", 8, known.at[3])
    one_hot_back(1, GT)

    for a, i in order[12:]:
        loads[a, i].wait()
    zero = jnp.zeros((8, 128), F32)
    sums = (zero, zero, zero)
    for i in (1, 2):
        prepare(i)

        def middle(c, acc, i=i):
            mid, out, inner, here = stencil(B, i, c)
            W[i, inner, :] = out
            return acc[0] + fold(mid * mid), acc[1] + fold(mid * out), acc[2] + fold(out * out)

        sums = lax.fori_loop(0, CY // ROWS, middle, sums)
    for c in w_inner:
        c.start()
    hear("sub", 8, known.at[3])
    hear("blk", 4, known.at[6])
    for peer in row:
        pl.semaphore_signal(known.at[7], inc=1, device_id=peer, device_id_type=MESH)
    wv = energy(1, True)(zero)
    wv = energy(2, False)(wv)

    right_one, left_one = has_right.astype(F32), has_left.astype(F32)
    most, rest = slice(0, NFB - CY), slice(NFB - CY, NFB)

    def gather_right(quarters, at):
        for rows, ys, cols, _ in pieces(quarters):
            HL[rows, :] = split(face_in[ys, cols])
        return jnp.dot(GL[:, at], HL[at, :], preferred_element_type=F32)

    def jumps_left(quarters, at):
        for rows, ys, cols, _ in pieces(quarters):
            jump = left_one * live_of(1, rows) * (last_in[ys, cols] - J1R[rows, :])
            HJ[rows, :] = split(jump)
            C2R[rows, :] = PENALTY * jump - psf[rows, :]
        HL2[at, :] = split(project(HJ[at, :], wpp, 1, at))
        return jnp.dot(GT[:, at], HL2[at, :], preferred_element_type=F32)

    first_left[0].wait_recv()
    last_right[0].wait_recv()
    ACC[...] = gather_right((0, 1, 2), most)
    g = jumps_left((0, 1, 2), most)
    for at, _, cols, ys in pieces(range(GROUPS)):
        W[0, ys, cols] = W[0, ys, cols] - PENALTY * (g[at, :FB] + g[at, FB:])
    first_left[1].wait_recv()
    last_right[1].wait_recv()
    g = jumps_left((3,), rest)
    for at, _, cols, ys in pieces(range(GROUPS)):
        w = W[0, ys, cols] - PENALTY * (g[at, :FB] + g[at, FB:])
        W[0, ys, cols] = w
        mid = B[0, ys, cols]
        sums = sums[0] + fold(mid * mid), sums[1] + fold(mid * w), sums[2] + fold(w * w)
    for c in w_first:
        c.start()
    g = ACC[...] + gather_right((3,), rest)
    projected = project(g.astype(BF16), wpt, 0)
    for at, _, cols, ys in pieces(range(GROUPS)):
        mid = B[3, ys, cols]
        jump = live_of(0, at) * (mid - projected[at])
        w = W[3, ys, cols] + PENALTY * jump
        W[3, ys, cols] = w
        HL[at, :] = split(jump)
        C2L[at, :] = w
        sums = sums[0] + fold(mid * mid), sums[1] + fold(mid * w), sums[2] + fold(w * w)

    for c in w_last:
        c.start()

    C2L[...] = C2L[...] + (PENALTY * right_one) * project(HL[...], wm, 0)
    C2R[...] = C2R[...] + PENALTY * project(HJ[...], wm, 1)
    wv = energy(0, True)(wv)
    wv = energy(3, False)(wv)

    def left_jump(q, wait=True):
        at = slice(q * CY, (q + 1) * CY)
        if wait:
            psf_left[q].wait_recv()
        return live_of(0, at) * (C2L[at, :] - psf_in[at, :])

    def right_jump(q, wait=True):
        at = slice(q * CY, (q + 1) * CY)
        if wait:
            sl_right[q].wait_recv()
        return left_one * live_of(1, at) * (sl_in[at, :] + C2R[at, :])

    def add_left(q, jump):
        for at, ys, cols, _ in pieces((q,)):
            V[3, ys, cols] = V[3, ys, cols] + PENALTY * jump[at.start - q * CY : at.stop - q * CY]

    def add_right(pair, at):
        back = split(project(pair, wpp, 1, at))
        g = jnp.dot(GT[:, at], back, preferred_element_type=F32)
        for rows, ys, cols, _ in pieces(range(GROUPS)):
            V[0, ys, cols] = V[0, ys, cols] - PENALTY * (g[rows, :FB] + g[rows, FB:])

    mortar = zero
    for q in (2, 3):
        at = slice(q * CY, (q + 1) * CY)
        only = live_of(0, at) * C2L[at, :]
        mortar = mortar + (1.0 - right_one) * fold(only * only)
    pl.semaphore_wait(known.at[7], n_blk - 1)
    for c in w_inner + w_first + w_last:
        c.wait_recv()
    across = jnp.zeros((1, CZ), F32)
    for i in range(CX):
        d = W[i, PAD + CY - 1 : PAD + CY, :] - edges[4, i, 0:1, :]
        across = across + TY[i, PAD + CY - 1 : PAD + CY, :] * d * d
        W[i, PAD - 1 : PAD, :] = edges[3, i, 0:1, :]
        W[i, PAD + CY : PAD + CY + 1, :] = edges[4, i, 0:1, :]
    lane_row = lax.broadcasted_iota(I32, (1, FB), 1)
    packed = jnp.zeros((1, FB), F32)
    for n, part in enumerate(sums):
        packed = jnp.where(lane_row == n, jnp.sum(part), packed)
    packed = jnp.where(lane_row == 3, jnp.sum(wv) + jnp.sum(across), packed)
    for n in range(2):
        jump = left_jump(n)
        mortar = mortar + fold(jump * jump)
        jump = right_jump(2 + n)
        mortar = mortar + fold(jump * jump)

    def spread(stage, part, peers):
        cur[stage, 0:1, :] = part
        for n, peer in enumerate(peers):
            pltpu.make_async_remote_copy(
                src_ref=cur.at[stage, 0:1], dst_ref=slots.at[stage, n : n + 1],
                send_sem=ar_ss.at[stage], recv_sem=ar_rs.at[stage], device_id=peer, device_id_type=MESH,
            ).start()

    def collect(stage, peers):
        arrived = slots.at[stage, 0 : len(peers)]
        pltpu.make_async_copy(arrived, arrived, ar_rs.at[stage]).wait()
        return cur[stage, 0:1, :] + jnp.sum(slots[stage, 0 : len(peers), :], axis=0, keepdims=True)

    spread(0, jnp.where(lane_row == 3, packed + PENALTY * jnp.sum(mortar), packed), plane)

    for q in (0, 1):
        sl_right[q].start()
        psf_left[q + 2].start()

    for i in range(CX):
        def second(c, _, i=i):
            mid, out, inner, here = stencil(W, i, c)
            V[i, here, :] = out
            return 0

        lax.fori_loop(0, CY // ROWS, second, 0)

    for q in (0, 1):
        add_left(q, left_jump(q, wait=False))
    add_right(jnp.concatenate([split(right_jump(q, wait=False)) for q in (2, 3)], axis=0), slice(2 * CY, 4 * CY))

    spread(1, collect(0, plane), in_line)

    for q in (2, 3):
        add_left(q, left_jump(q))
        add_right(split(right_jump(q - 2)), slice((q - 2) * CY, (q - 1) * CY))

    total = collect(1, in_line)
    bb, bw, ww, wv = (total[0:1, n : n + 1] for n in range(4))
    alpha = bb / bw
    rr = alpha * alpha * ww - bb
    beta = rr / bb
    curve = bw - 2.0 * alpha * ww + alpha * alpha * wv - beta * beta * bw
    alpha2 = rr / curve
    scalars[0:8, :] = jnp.broadcast_to(alpha + alpha2 * (1.0 + beta), (8, 128))
    scalars[8:16, :] = jnp.broadcast_to(alpha * alpha2, (8, 128))

    for c in pairs_right + [b_up, b_down, ty_up] + w_inner + w_first + w_last + first_left + last_right + sl_right + psf_left:
        c.wait_send()
    for stage, peers in enumerate((plane, in_line)):
        sent = slots.at[stage, 0 : len(peers)]
        pltpu.make_async_copy(sent, sent, ar_ss.at[stage]).wait()


def finish_kernel(B, W, V, scalars, x_hbm, r_hbm, x_v, r_v, sem):
    first, cross = scalars[0:1, 0:1], scalars[8:9, 0:1]
    out = []
    for i in range(CX):
        for h in range(2):
            n = 2 * i + h
            here, inner = pl.ds(h * ROWS, ROWS), pl.ds(PAD + h * ROWS, ROWS)
            b, w = B[i, inner, :], W[i, inner, :]
            x_v[i, here, :] = first * b - cross * w
            out.append(pltpu.make_async_copy(x_v.at[i, here], x_hbm.at[i, here], sem.at[0, n]))
            out[-1].start()
            r_v[i, here, :] = b - first * w + cross * V[i, here, :]
            out.append(pltpu.make_async_copy(r_v.at[i, here], r_hbm.at[i, here], sem.at[1, n]))
            out[-1].start()
    for c in out:
        c.wait()


def body(mesh, b, tx, ty, tz, st, perm, kind, count, proj):
    n_sub, n_blk = mesh.shape["sub"], mesh.shape["blk"]
    vm = lambda *shape, dtype=F32: pltpu.VMEM(shape, dtype)
    face, block, padded = (NFB, FB), (CX, CY, CZ), (CX, CY + 2 * PAD, CZ)
    scratch = [
        vm(*block), vm(CX, CY + PAD, CZ), vm(*block), vm(*block),
        vm(1, 1, NFB, dtype=I32), vm(1, 1, NFB, dtype=I32),
        vm(8, FB, dtype=I32),
        vm(1, 1, NFB, dtype=I32), vm(1, 1, NFB, dtype=I32), vm(8, FB, dtype=I32), vm(KINDS, FB, FB),
        vm(6 * FB, 2 * FB, dtype=BF16), vm(6 * FB, 2 * FB, dtype=BF16), vm(6 * FB, 2 * FB, dtype=BF16),
        vm(2, NFB, FB, dtype=I32), vm(2, NFB, FB, dtype=BF16), vm(*face),
        vm(NFB, NFB, dtype=BF16), vm(NFB, NFB, dtype=BF16), vm(NFB, NFB, dtype=BF16),
        vm(CY, CZ), vm(CY, CZ), vm(*face), vm(*face), vm(*face), vm(*face),
        vm(NFB, 2 * FB, dtype=BF16), vm(NFB, 2 * FB, dtype=BF16), vm(NFB, 2 * FB, dtype=BF16), vm(NFB, 2 * FB),
        vm(*face), vm(*face), vm(*face),
        vm(5, CX, 8, CZ), vm(2, 8, FB), vm(2, 32, FB), pltpu.SemaphoreType.REGULAR((8,)),
        pltpu.SemaphoreType.DMA((5, CX)), pltpu.SemaphoreType.DMA((3,)),
        pltpu.SemaphoreType.DMA((24,)), pltpu.SemaphoreType.DMA((24,)),
        pltpu.SemaphoreType.DMA((2,)), pltpu.SemaphoreType.DMA((2,)),
    ]
    like = lambda *shape: jax.ShapeDtypeStruct(shape, F32)
    in_vmem, in_hbm = pl.BlockSpec(memory_space=pltpu.VMEM), pl.BlockSpec(memory_space=pltpu.HBM)
    args = [pltpu.with_memory_space_constraint(a, pltpu.HBM) for a in (b, tx, ty, tz, st, perm, kind, proj)]
    state = pl.pallas_call(
        functools.partial(kernel, n_sub, n_blk),
        out_shape=(vm(*padded), vm(*padded), vm(*block), vm(16, 128)),
        in_specs=[in_hbm] * 8 + [pl.BlockSpec(memory_space=pltpu.SMEM)],
        out_specs=(in_vmem,) * 4,
        scratch_shapes=scratch,
        compiler_params=pltpu.CompilerParams(
            collective_id=0, has_side_effects=True, vmem_limit_bytes=48 * 1024 * 1024
        ),
        name="darcy_cg",
    )(*args, count)
    return tuple(pl.pallas_call(
        finish_kernel,
        out_shape=(like(*block), like(*block)),
        in_specs=[in_vmem] * 4,
        out_specs=(in_hbm,) * 2,
        scratch_shapes=[vm(*block), vm(*block), pltpu.SemaphoreType.DMA((2, 2 * CX))],
        compiler_params=pltpu.CompilerParams(vmem_limit_bytes=32 * 1024 * 1024),
        name="finish",
    )(*state))


def solution(mesh):
    cells = P("sub", "blk", None)
    return jax.shard_map(
        functools.partial(body, mesh), mesh=mesh,
        in_specs=(cells,) * 7 + (P("sub", "blk"), P()), out_specs=(cells, cells), check_vma=False,
    )
```
